256 devices in a mesh: ens: 16 (over y, x_hi, core), lat: 16 (over x_lo, z).
Axes of the slice: x: 4 (x_hi: 2, x_lo: 2; x = x_hi * 2 + x_lo), y: 4, z: 8, core: 2. Of those that a mesh axis runs over, the one named last changes fastest.
Arguments:
- grid: bfloat16 [16, 8, 512, 1440], P('ens', None, 'lat'), may hold values from -48 to 48
- legendre: bfloat16 [512, 384, 384], P('lat'), as said below
- target: float32 [384, 8, 2, 384], P('lat'), may hold values from -6 to 6
- owner: int32 [384], replicated, may hold values from 0 to 383, each once
- cutoff: int32 [8], replicated, may hold values from 90 to 360
Outputs:
- mean_score: float32 [1], replicated
- score_grad: bfloat16 [16, 8, 512, 1440], P('ens', None, 'lat')
The draws below stay inside these ranges and needn't reach their ends.
Inputs may be any that keep to these rules, and one draw needn't show every extreme that they name: legendre is zero where l < m or l > 360. owner names each order 0 to 383 once; index j of lat owns slots j * 384 / 16 onward.
All inputs are finite; a program needn't handle non-finite values.
Results may differ from the reference program's by a relative error of at most 0.0075.
The reference program's roundings to bfloat16 on the way (of `waves`, `fourier`, `coeff_grad` and `fourier_grad`) count: a program that leaves them out, or rounds other values in their place, can miss the bound.
Values may be sent and summed in bfloat16 or wider, within the bound.
No kernel may reach another device: no remote copies, remote signals or barrier semaphores. Data moves between devices by JAX's collectives and lax.ppermute only.
A program may use at most 128 MiB of HBM per device.

```python
import math
import jax
import jax.numpy as jnp

F = 8
NLON = 1440
LMAX = 360
L_PAD = 384
M_PAD = 384
ENSEMBLE = 16
NLAT = 512


def member_scales(top):
    steps = jnp.arange(ENSEMBLE, dtype=jnp.float32) / jnp.float32(max(ENSEMBLE - 1, 1))
    return jnp.exp(steps * jnp.log(jnp.float32(top)))[:, None, None, None]


def draw_grid(key, part):
    key = jax.random.fold_in(key, 5)
    shape = (ENSEMBLE, F, NLAT, NLON)
    values = jnp.clip(jax.random.normal(key, shape, jnp.float32), -6.0, 6.0) * member_scales(4.0)
    return values.astype(jnp.bfloat16)


def draw_legendre(key, part):
    key = jax.random.fold_in(key, 11)
    values = jax.random.normal(key, (NLAT, M_PAD, L_PAD), jnp.float32) / jnp.sqrt(jnp.float32(NLAT))
    orders = jnp.arange(M_PAD, dtype=jnp.int32)[:, None]
    degrees = jnp.arange(L_PAD, dtype=jnp.int32)[None, :]
    nonzero = ((degrees >= orders) & (degrees <= LMAX)).astype(jnp.float32)
    return (values * nonzero[None]).astype(jnp.bfloat16)


def place_ends(values, key, low, largest):
    longest = values.shape.index(max(values.shape))
    spots = []
    for shift in (0, 1):
        where = [jax.random.randint(jax.random.fold_in(key, axis), (), 0, length) for axis, length in enumerate(values.shape)]
        where[longest] = (where[longest] + shift) % values.shape[longest]
        spots.append(tuple(where))
    return values.at[spots[0]].set(low).at[spots[1]].set(largest)


def block_levels(key, shape, cuts, smallest, largest):
    loudness = 1.0
    for dim, blocks in cuts:
        heights = jax.random.uniform(jax.random.fold_in(jax.random.fold_in(key, 6), dim), (blocks,), jnp.float32, smallest / len(cuts), largest / len(cuts))
        loudness = loudness * jnp.repeat(jnp.exp(heights), shape[dim] // blocks).reshape((-1,) + (1,) * (len(shape) - 1 - dim))
    return loudness


def centred(rng, extent, scale, most, pieces=(), kind=jnp.bfloat16):
    loudness = block_levels(rng, extent, pieces, -0.22, 0.18) if pieces else 1.0
    drawn = jax.random.normal(rng, extent, jnp.float32) * scale * loudness
    return jnp.minimum(jnp.maximum(drawn, -most), most).astype(kind)


def setup_inputs(seed: int = 0) -> dict:
    streams_of = jax.random.split(jax.random.key(seed), 6)
    grid = draw_grid(jax.random.fold_in(streams_of[5], 71), 0)
    legendre = draw_legendre(jax.random.fold_in(streams_of[5], 71), 0)
    target = centred(streams_of[2], (M_PAD, F, 2, L_PAD), 1.0, 6.0, ((0, 16),), jnp.float32)
    owner = jax.random.permutation(streams_of[3], M_PAD).astype(jnp.int32)
    cutoff = place_ends(jax.random.randint(streams_of[4], (F,), LMAX // 4, LMAX + 1), jax.random.fold_in(streams_of[4], 1), LMAX // 4, LMAX).astype(jnp.int32)
    return {"grid": grid, "legendre": legendre, "target": target, "owner": owner, "cutoff": cutoff}


delta_abs = 0.1

def wave_table(modes, lon_count):
    points = jnp.arange(lon_count, dtype=jnp.int32)
    phase = points[:, None] * modes[None, :] % lon_count
    angle = phase.astype(jnp.float32) * (2.0 * math.pi / lon_count)
    both = jnp.stack([jnp.cos(angle), -jnp.sin(angle)], axis=1) / math.sqrt(lon_count)
    return both.astype(jnp.bfloat16)

def smooth_abs(spread):
    return jnp.sqrt(spread * spread + delta_abs * delta_abs) - delta_abs

def abs_slope(spread):
    return spread / jnp.sqrt(spread * spread + delta_abs * delta_abs)

def reference(grid, legendre, target, owner, cutoff):
    natural = jnp.arange(M_PAD, dtype=jnp.int32)
    waves = wave_table(natural, NLON)
    fourier = jnp.einsum('efan,nck->efack', grid.astype(jnp.float32), waves.astype(jnp.float32)).astype(jnp.bfloat16)
    weights = legendre.astype(jnp.float32)
    coeffs_nat = jnp.einsum('efack,akl->kefcl', fourier.astype(jnp.float32), weights)
    coeffs = jnp.take(coeffs_nat, owner, axis=0)
    levels = jnp.arange(L_PAD, dtype=jnp.int32)
    inside = ((levels[None, None, :] >= owner[:, None, None]) & (levels[None, None, :] <= cutoff[None, :, None])).astype(jnp.float32)
    mode_mask = inside[:, None, :, None, :]
    target_rows = target[:, None]
    pair_value = jnp.zeros_like(coeffs)
    pair_slope = jnp.zeros_like(coeffs)
    for member in range(ENSEMBLE):
        spread = coeffs - coeffs[:, member:member + 1]
        pair_value = pair_value + smooth_abs(spread)
        pair_slope = pair_slope + abs_slope(spread)
    own_value = smooth_abs(coeffs - target_rows)
    own_slope = abs_slope(coeffs - target_rows)
    score_sum = jnp.sum(mode_mask * (own_value / ENSEMBLE - pair_value / (2.0 * ENSEMBLE * ENSEMBLE)))
    cut_level = cutoff.astype(jnp.float32)
    modes_valid = jnp.sum((cut_level + 1.0) * (cut_level + 2.0))
    coeff_grad = (mode_mask * (own_slope - pair_slope / ENSEMBLE)).astype(jnp.bfloat16)
    natural_grad = jnp.zeros_like(coeff_grad).at[owner].set(coeff_grad)
    fourier_grad = jnp.einsum('kefcl,akl->efack', natural_grad.astype(jnp.float32), weights).astype(jnp.bfloat16)
    grid_grad = jnp.einsum('efack,nck->efan', fourier_grad.astype(jnp.float32), waves.astype(jnp.float32)).astype(jnp.bfloat16)
    return ((score_sum / modes_valid).reshape(1), grid_grad)
```

```python
import functools
import math

import jax
import jax.numpy as jnp
import numpy as np
from jax import lax
from jax.experimental import pallas as pl
from jax.experimental.pallas import tpu as pltpu
from jax.sharding import PartitionSpec as P

delta_abs = 0.1
both_axes = ("lat", "ens")


def wave_table(mode_count, lon_count):
    points = np.arange(lon_count, dtype=np.int64)
    modes = np.arange(mode_count, dtype=np.int64)
    phase = modes[:, None] * points[None, :] % lon_count
    angle = phase.astype(np.float32) * np.float32(2.0 * math.pi / lon_count)
    both = np.stack([np.cos(angle), -np.sin(angle)]) / np.float32(math.sqrt(lon_count))
    return both.astype(np.float32).astype(jnp.bfloat16)


def score_kernel(
    orders_ref, first_ref, second_ref, weights_ref, target_ref, cutoff_ref,
    back_first_ref, back_second_ref, score_ref,
    rows_ref, tiled_ref, coeffs_ref, grads_ref,
):
    lane_field = lax.broadcasted_iota(jnp.int32, (16, 128), 1) // 32
    halves = (first_ref, second_ref)
    for j in range(16):
        for tile in range(6):
            source = halves[tile // 3]
            block = source[16 * j:16 * j + 16, 128 * (tile % 3):128 * (tile % 3) + 128]
            for k in range(4):
                row = (tile * 4 + k) * 16
                rows_ref[row:row + 16, 128 * j:128 * j + 128] = jnp.where(
                    lane_field == k, block, jnp.zeros_like(block)
                )
        band = weights_ref[32 * j:32 * j + 32, :]
        for k in range(4):
            tiled_ref[128 * j + 32 * k:128 * j + 32 * k + 32, :] = band
    full = jnp.dot(rows_ref[0:256, :], tiled_ref[:, 0:384], preferred_element_type=jnp.float32)
    half = jnp.dot(rows_ref[256:384, :], tiled_ref[:, 384:768], preferred_element_type=jnp.float32)
    for third in range(3):
        coeffs_ref[third, 0:256, :] = full[:, 128 * third:128 * third + 128]
        coeffs_ref[third, 256:384, :] = half[:, 128 * third:128 * third + 128]
    offset = delta_abs * delta_abs
    limit = cutoff_ref[...]
    total = jnp.zeros((8, 128), jnp.float32)

    def column(step, total):
        part = step // 3
        third = step % 3
        lanes = pl.ds(pl.multiple_of(third * 128, 128), 128)
        order = orders_ref[part]
        level = lax.broadcasted_iota(jnp.int32, (8, 128), 1) + third * 128
        inside = (level >= order) & (level <= limit)
        goal = target_ref[pl.ds(pl.multiple_of(part * 8, 8), 8), lanes]
        member = [
            coeffs_ref[third, pl.ds(part * 128 + e, 8, stride=16), :] for e in range(16)
        ]
        slope = [jnp.zeros((8, 128), jnp.float32) for _ in range(16)]
        pair_value = jnp.zeros((8, 128), jnp.float32)
        for i in range(16):
            for k in range(i + 1, 16):
                spread = member[i] - member[k]
                square = spread * spread + offset
                inverse = lax.rsqrt(square)
                step_slope = spread * inverse
                slope[i] = slope[i] + step_slope
                slope[k] = slope[k] - step_slope
                pair_value = pair_value + (square * inverse - delta_abs)
        own_value = jnp.zeros((8, 128), jnp.float32)
        for i in range(16):
            spread = member[i] - goal
            square = spread * spread + offset
            inverse = lax.rsqrt(square)
            own_value = own_value + (square * inverse - delta_abs)
            grad = spread * inverse - slope[i] / 16.0
            grads_ref[third, pl.ds(part * 128 + i, 8, stride=16), :] = jnp.where(inside, grad, 0.0)
        value = own_value / 16.0 - pair_value / 256.0
        return total + jnp.where(inside, value, 0.0)

    total = lax.fori_loop(0, 9, column, total)
    score = jnp.sum(jnp.sum(total, axis=1, keepdims=True), axis=0, keepdims=True)
    high = score.astype(jnp.bfloat16)
    rest = score - high.astype(jnp.float32)
    middle = rest.astype(jnp.bfloat16)
    low = (rest - middle.astype(jnp.float32)).astype(jnp.bfloat16)
    spot = lax.broadcasted_iota(jnp.int32, (256, 128), 1)
    pieces = jnp.where(
        spot == 0, high.astype(jnp.float32),
        jnp.where(spot == 1, middle.astype(jnp.float32), low.astype(jnp.float32)),
    )
    score_ref[...] = jnp.where(spot < 3, pieces, 0.0).astype(jnp.bfloat16)

    backs = (back_first_ref, back_second_ref)
    lane_wide = lax.broadcasted_iota(jnp.int32, (16, 2048), 1) // 32 % 4
    for tile in range(6):
        weights = tiled_ref[:, 0:384] if tile < 4 else tiled_ref[:, 384:768]
        grads = jnp.concatenate(
            [grads_ref[third, tile * 64:tile * 64 + 64, :] for third in range(3)], axis=1
        ).astype(jnp.bfloat16)
        wide = lax.dot_general(
            grads, weights, (((1,), (1,)), ((), ())), preferred_element_type=jnp.float32
        )
        merged = wide[0:16]
        for k in range(1, 4):
            merged = jnp.where(lane_wide == k, wide[16 * k:16 * k + 16], merged)
        merged = merged.astype(jnp.bfloat16)
        target_half = backs[tile // 3]
        for j in range(16):
            target_half[16 * j:16 * j + 16, 128 * (tile % 3):128 * (tile % 3) + 128] = merged[
                :, 128 * j:128 * j + 128
            ]


def score_call(orders, first, second, weights, target_rows, limit):
    vmem = pl.BlockSpec(memory_space=pltpu.VMEM)
    return pl.pallas_call(
        score_kernel,
        out_shape=(
            jax.ShapeDtypeStruct((256, 384), jnp.bfloat16),
            jax.ShapeDtypeStruct((256, 384), jnp.bfloat16),
            jax.ShapeDtypeStruct((256, 128), jnp.bfloat16),
        ),
        in_specs=[pl.BlockSpec(memory_space=pltpu.SMEM), vmem, vmem, vmem, vmem, vmem],
        out_specs=(vmem, vmem, vmem),
        scratch_shapes=[
            pltpu.VMEM((384, 2048), jnp.bfloat16),
            pltpu.VMEM((2048, 768), jnp.bfloat16),
            pltpu.VMEM((3, 384, 128), jnp.float32),
            pltpu.VMEM((3, 384, 128), jnp.float32),
        ],
        compiler_params=pltpu.CompilerParams(vmem_limit_bytes=40 * 1024 * 1024),
    )(orders, first, second, weights, target_rows, limit)


def exact_dot(left, right, dims=((1,), (0,))):
    return lax.dot_general(
        left, right, (dims, ((), ())), preferred_element_type=jnp.float32
    ).astype(jnp.bfloat16)


def body(grid, legendre, target, owner, cutoff):
    fields, rows, lon_count = grid.shape[1:]
    modes = legendre.shape[1]
    e = lax.axis_index("ens")
    j = lax.axis_index("lat")
    waves = jnp.asarray(wave_table(modes, lon_count).reshape(2 * modes, lon_count))
    by_lat = owner.reshape(16, 24)
    order_full = by_lat[:, :16].reshape(256)
    order_half = jnp.repeat(by_lat[:, 16:], 2, axis=1).reshape(256)
    parity = jnp.arange(256, dtype=jnp.int32) % 2
    natural = jnp.arange(modes, dtype=jnp.int32)
    pick_full = (order_full[:, None] == natural).astype(jnp.bfloat16)
    pick_half = (order_half[:, None] == natural).astype(jnp.bfloat16)
    both = jnp.arange(2 * modes, dtype=jnp.int32)
    pick_side = ((order_half + modes * parity)[:, None] == both).astype(jnp.bfloat16)

    fourier = exact_dot(waves, grid.reshape(fields * rows, lon_count), ((1,), (1,)))
    part0 = exact_dot(pick_full, fourier[:modes])
    part1 = exact_dot(pick_full, fourier[modes:])
    part2 = exact_dot(pick_side, fourier)
    bands = lax.dynamic_slice_in_dim(legendre, 2 * e, 2, axis=0)
    sent = jnp.stack(
        [
            jnp.concatenate(
                [part0, part1[:, :128], exact_dot(pick_full, bands[0]), exact_dot(pick_half, bands[0])], axis=1
            ),
            jnp.concatenate(
                [part1[:, 128:], part2, exact_dot(pick_full, bands[1]), exact_dot(pick_half, bands[1])], axis=1
            ),
        ],
        axis=1,
    )
    got = lax.all_to_all(sent, both_axes, split_axis=0, concat_axis=0, tiled=True)

    weights = got[:, :, 384:].reshape(512, 768)
    full_slot = e
    half_slot = 16 + e // 2
    side = e % 2
    own_orders = lax.dynamic_slice_in_dim(owner, 24 * j, 24)
    orders = jnp.stack([own_orders[full_slot], own_orders[full_slot], own_orders[half_slot]])
    full_rows = lax.dynamic_index_in_dim(target, full_slot, 0, keepdims=False)
    half_rows = lax.dynamic_slice(target, (half_slot, 0, side, 0), (1, fields, 1, target.shape[3]))
    target_rows = jnp.concatenate([full_rows[:, 0], full_rows[:, 1], half_rows[0, :, 0]])
    limit = jnp.broadcast_to(cutoff[:, None], (fields, 128))
    back0, back1, score = score_call(
        orders, got[:, 0, :384], got[:, 1, :384], weights, target_rows, limit
    )
    returned = jnp.stack(
        [jnp.concatenate([back0, score], axis=1), jnp.concatenate([back1, score], axis=1)], axis=1
    )
    home = lax.all_to_all(returned, both_axes, split_axis=0, concat_axis=0, tiled=True)
    score_sum = jnp.sum(home[:, 0, 384:387].astype(jnp.float32))
    cut_level = cutoff.astype(jnp.float32)
    modes_valid = jnp.sum((cut_level + 1.0) * (cut_level + 2.0))
    mean_score = (score_sum / modes_valid).reshape(1)

    grad0 = home[:, 0, :256]
    grad1 = jnp.concatenate([home[:, 0, 256:384], home[:, 1, :128]], axis=1)
    grad2 = home[:, 1, 128:384]
    chosen = jnp.concatenate([grad0, grad1, grad2])
    zeros = jnp.zeros_like(pick_full)
    spread_all = jnp.concatenate(
        [
            jnp.concatenate([pick_full, zeros], axis=1),
            jnp.concatenate([zeros, pick_full], axis=1),
            pick_side,
        ]
    )
    natural_grad = exact_dot(spread_all, chosen, ((0,), (0,)))
    grid_grad = exact_dot(natural_grad, waves, ((0,), (0,)))
    return (mean_score, grid_grad.reshape(1, fields, rows, lon_count))


def solution(mesh):
    in_specs = (
        P("ens", None, "lat", None),
        P("lat", None, None),
        P("lat", None, None, None),
        P(),
        P(),
    )
    out_specs = (P(), P("ens", None, "lat", None))
    return jax.shard_map(body, mesh=mesh, in_specs=in_specs, out_specs=out_specs, check_vma=False)
```

```python
import math

import jax
import jax.numpy as jnp
import numpy as np
from jax import lax
from jax.experimental import pallas as pl
from jax.experimental.pallas import tpu as pltpu
from jax.sharding import PartitionSpec as P

delta_abs = 0.1
both_axes = ("lat", "ens")


def wave_table(mode_count, lon_count):
    points = np.arange(lon_count, dtype=np.int64)
    modes = np.arange(mode_count, dtype=np.int64)
    phase = modes[:, None] * points[None, :] % lon_count
    angle = phase.astype(np.float32) * np.float32(2.0 * math.pi / lon_count)
    both = np.stack([np.cos(angle), -np.sin(angle)]) / np.float32(math.sqrt(lon_count))
    return both.astype(np.float32).astype(jnp.bfloat16)


def column_of(codes_ref, row):
    line = codes_ref[row:row + 1, :]
    return jnp.transpose(jnp.broadcast_to(line, (128, 512)), (1, 0))

def pick_rows(codes_ref, row):
    column = column_of(codes_ref, row)
    lane = lax.broadcasted_iota(jnp.int32, (512, 128), 1).astype(jnp.float32)
    return jnp.concatenate(
        [jnp.where(column == lane + 128.0 * t, 1.0, 0.0).astype(jnp.bfloat16) for t in range(6)], axis=1)

def send_kernel(codes_ref, grid_ref, waves_ref, bands_ref, out_ref, four_ref):
    four_ref[...] = lax.dot_general(waves_ref[...], grid_ref[...], (((1,), (1,)), ((), ())),
        preferred_element_type=jnp.float32).astype(jnp.bfloat16)
    full = pick_rows(codes_ref, 0)
    half = pick_rows(codes_ref, 1)
    side = pick_rows(codes_ref, 2)
    dot = lambda a, b: jnp.dot(a, b, preferred_element_type=jnp.float32)
    out_ref[:, 0:256] = dot(full, four_ref[...]).astype(jnp.bfloat16)
    out_ref[:, 384:768] = dot(full, bands_ref[...]).astype(jnp.bfloat16)
    out_ref[:, 768:1152] = dot(half, bands_ref[...]).astype(jnp.bfloat16)
    both = dot(side, four_ref[...])
    odd = lax.broadcasted_iota(jnp.int32, (512, 128), 0) % 2
    out_ref[:, 256:384] = jnp.where(odd == 0, both[:, :128], both[:, 128:]).astype(jnp.bfloat16)

def send_call(codes, grid, waves, bands):
    vm = pl.BlockSpec(memory_space=pltpu.VMEM)
    return pl.pallas_call(send_kernel, out_shape=jax.ShapeDtypeStruct((512, 1152), jnp.bfloat16),
        in_specs=[vm]*4, out_specs=vm, scratch_shapes=[pltpu.VMEM((768, 256), jnp.bfloat16)],
        compiler_params=pltpu.CompilerParams(vmem_limit_bytes=40*1024*1024))(codes, grid, waves, bands)

def home_kernel(codes_ref, got_ref, waves_ref, out_ref):
    row = lax.broadcasted_iota(jnp.int32, (768, 512), 0).astype(jnp.float32)
    full = jnp.where(row == codes_ref[0:1, :], 1.0, 0.0).astype(jnp.bfloat16)
    side = jnp.where(row == codes_ref[2:3, :], 1.0, 0.0).astype(jnp.bfloat16)
    odd = lax.broadcasted_iota(jnp.int32, (512, 128), 0) % 2
    third = got_ref[:, 256:384]
    zero = jnp.zeros_like(third)
    wide = jnp.concatenate([jnp.where(odd == 0, third, zero), jnp.where(odd == 1, third, zero)], axis=1)
    natural = (jnp.dot(full, got_ref[:, 0:256], preferred_element_type=jnp.float32)
        + jnp.dot(side, wide, preferred_element_type=jnp.float32)).astype(jnp.bfloat16)
    out_ref[...] = lax.dot_general(natural, waves_ref[...], (((0,), (0,)), ((), ())),
        preferred_element_type=jnp.float32).astype(jnp.bfloat16)

def home_call(codes, got, waves):
    vm = pl.BlockSpec(memory_space=pltpu.VMEM)
    return pl.pallas_call(home_kernel, out_shape=jax.ShapeDtypeStruct((256, 1440), jnp.bfloat16),
        in_specs=[vm]*3, out_specs=vm,
        compiler_params=pltpu.CompilerParams(vmem_limit_bytes=40*1024*1024))(codes, got, waves)

def score_kernel(orders_ref, got_ref, target_ref, cutoff_ref, back_ref,
                 rows_ref, tiled_ref, coeffs_ref, grads_ref, wide_ref):
    lane_field = lax.broadcasted_iota(jnp.int32, (32, 128), 1) // 32
    for j in range(16):
        for q in range(3):
            block = got_ref[32 * j:32 * j + 32, 128 * q:128 * q + 128]
            for k in range(4):
                row = (q * 4 + k) * 32
                rows_ref[row:row + 32, 128 * j:128 * j + 128] = jnp.where(
                    lane_field == k, block, jnp.zeros_like(block))
        band = got_ref[32 * j:32 * j + 32, 384:1152]
        for k in range(4):
            tiled_ref[128 * j + 32 * k:128 * j + 32 * k + 32, :] = band
    full = jnp.dot(rows_ref[0:256, :], tiled_ref[:, 0:384], preferred_element_type=jnp.float32)
    half = jnp.dot(rows_ref[256:384, :], tiled_ref[:, 384:768], preferred_element_type=jnp.float32)
    for third in range(3):
        coeffs_ref[third, 0:256, :] = full[:, 128 * third:128 * third + 128]
        coeffs_ref[third, 256:384, :] = half[:, 128 * third:128 * third + 128]
    offset = delta_abs * delta_abs
    limit = cutoff_ref[...]

    def column(third, part, order, load, store):
        lanes = pl.ds(pl.multiple_of(third * 128, 128), 128)
        level = lax.broadcasted_iota(jnp.int32, (8, 128), 1) + third * 128
        inside = (level >= order) & (level <= limit)
        goal = target_ref[pl.ds(pl.multiple_of(part * 8, 8), 8), lanes]
        member = [load(e) for e in range(16)]
        slope = [jnp.zeros((8, 128), jnp.float32) for _ in range(16)]
        pair_value = jnp.zeros((8, 128), jnp.float32)
        for i in range(16):
            for k in range(i + 1, 16):
                spread = member[i] - member[k]
                square = spread * spread + offset
                inverse = lax.rsqrt(square)
                step_slope = spread * inverse
                slope[i] = slope[i] + step_slope
                slope[k] = slope[k] - step_slope
                pair_value = pair_value + (square * inverse - delta_abs)
        own_value = jnp.zeros((8, 128), jnp.float32)
        for i in range(16):
            spread = member[i] - goal
            square = spread * spread + offset
            inverse = lax.rsqrt(square)
            own_value = own_value + (square * inverse - delta_abs)
            grad = spread * inverse - slope[i] / 16.0
            store(i, jnp.where(inside, grad, 0.0))
        return jnp.where(inside, own_value / 16.0 - pair_value / 256.0, 0.0)

    def full_column(step, total):
        part = step // 3
        third = step % 3
        def load(e):
            return coeffs_ref[third, pl.ds(2 * e + part, 8, stride=32), :]
        def store(e, value):
            grads_ref[third, pl.ds(2 * e + part, 8, stride=32), :] = value
        return total + column(third, part, orders_ref[0], load, store)

    def half_column(third, total):
        def load(e):
            return jnp.concatenate([coeffs_ref[third, pl.ds(256 + 2 * e + h, 4, stride=32), :] for h in range(2)])
        def store(e, value):
            for h in range(2):
                grads_ref[third, pl.ds(256 + 2 * e + h, 4, stride=32), :] = value[4 * h:4 * h + 4]
        return total + column(third, 2, orders_ref[1], load, store)

    total = lax.fori_loop(0, 6, full_column, jnp.zeros((8, 128), jnp.float32))
    total = lax.fori_loop(0, 3, half_column, total)
    score = jnp.sum(jnp.sum(total, axis=1, keepdims=True), axis=0, keepdims=True)
    high = score.astype(jnp.bfloat16).astype(jnp.float32)
    middle = (score - high).astype(jnp.bfloat16).astype(jnp.float32)
    low = score - high - middle
    spot = lax.broadcasted_iota(jnp.int32, (512, 128), 1)
    pieces = jnp.where(spot == 0, high, jnp.where(spot == 1, middle, jnp.where(spot == 2, low, 0.0)))
    back_ref[:, 384:512] = pieces.astype(jnp.bfloat16)

    grads = jnp.concatenate([grads_ref[third] for third in range(3)], axis=1).astype(jnp.bfloat16)
    dims = (((1,), (1,)), ((), ()))
    wide_ref[0:256, :] = lax.dot_general(grads[0:256], tiled_ref[:, 0:384], dims, preferred_element_type=jnp.float32)
    wide_ref[256:384, :] = lax.dot_general(grads[256:384], tiled_ref[:, 384:768], dims, preferred_element_type=jnp.float32)
    for j in range(16):
        for q in range(3):
            merged = wide_ref[q * 128:q * 128 + 32, 128 * j:128 * j + 128]
            for k in range(1, 4):
                row = (q * 4 + k) * 32
                merged = jnp.where(lane_field == k, wide_ref[row:row + 32, 128 * j:128 * j + 128], merged)
            back_ref[32 * j:32 * j + 32, 128 * q:128 * q + 128] = merged.astype(jnp.bfloat16)

def score_call(orders, got, target_rows, limit):
    vm = pl.BlockSpec(memory_space=pltpu.VMEM)
    return pl.pallas_call(score_kernel, out_shape=jax.ShapeDtypeStruct((512, 512), jnp.bfloat16),
        in_specs=[pl.BlockSpec(memory_space=pltpu.SMEM), vm, vm, vm], out_specs=vm,
        scratch_shapes=[pltpu.VMEM((384, 2048), jnp.bfloat16), pltpu.VMEM((2048, 768), jnp.bfloat16),
            pltpu.VMEM((3, 384, 128), jnp.float32), pltpu.VMEM((3, 384, 128), jnp.float32),
            pltpu.VMEM((384, 2048), jnp.float32)],
        compiler_params=pltpu.CompilerParams(vmem_limit_bytes=40*1024*1024))(orders, got, target_rows, limit)


def body(grid, legendre, target, owner, cutoff):
    fields, rows, lon_count = grid.shape[1:]
    modes = legendre.shape[1]
    e = lax.axis_index("ens")
    j = lax.axis_index("lat")
    waves = jnp.asarray(wave_table(modes, lon_count).reshape(2 * modes, lon_count))
    by_lat = owner.reshape(16, 24)
    order_full = jnp.repeat(by_lat[:, :16].reshape(256), 2)
    order_half = jnp.repeat(by_lat[:, 16:].reshape(128), 4)
    place = jnp.arange(512, dtype=jnp.int32)
    codes = jnp.stack([
        order_full + modes * (place % 2),
        order_half + modes * (place % 2),
        order_half + modes * (place // 2 % 2),
    ]).astype(jnp.float32)
    codes = jnp.concatenate([codes, jnp.zeros((5, 512), jnp.float32)])
    bands = lax.dynamic_slice_in_dim(legendre, 2 * e, 2, axis=0).reshape(2 * modes, -1)
    sent = send_call(codes, grid.reshape(fields * rows, lon_count), waves, bands)
    got = lax.all_to_all(
        sent.reshape(256, 2, 1152), both_axes, split_axis=0, concat_axis=0, tiled=True
    ).reshape(512, 1152)

    full_slot = e
    half_slot = 16 + e // 2
    side = e % 2
    own_orders = lax.dynamic_slice_in_dim(owner, 24 * j, 24)
    orders = jnp.stack([own_orders[full_slot], own_orders[half_slot]])
    full_rows = lax.dynamic_index_in_dim(target, full_slot, 0, keepdims=False)
    half_rows = lax.dynamic_slice(target, (half_slot, 0, side, 0), (1, fields, 1, target.shape[3]))
    target_rows = jnp.concatenate([full_rows[:, 0], full_rows[:, 1], half_rows[0, :, 0]])
    limit = jnp.broadcast_to(cutoff[:, None], (fields, 128))
    back = score_call(orders, got, target_rows, limit)
    home = lax.all_to_all(
        back.reshape(256, 2, 512), both_axes, split_axis=0, concat_axis=0, tiled=True
    ).reshape(512, 512)
    score_sum = jnp.sum(home[::2, 384:387].astype(jnp.float32))
    cut_level = cutoff.astype(jnp.float32)
    modes_valid = jnp.sum((cut_level + 1.0) * (cut_level + 2.0))
    mean_score = (score_sum / modes_valid).reshape(1)
    grid_grad = home_call(codes, home, waves)
    return (mean_score, grid_grad.reshape(1, fields, rows, lon_count))


def solution(mesh):
    in_specs = (
        P("ens", None, "lat", None),
        P("lat", None, None),
        P("lat", None, None, None),
        P(),
        P(),
    )
    out_specs = (P(), P("ens", None, "lat", None))
    return jax.shard_map(body, mesh=mesh, in_specs=in_specs, out_specs=out_specs, check_vma=False)
```

```python
import math

import jax
import jax.numpy as jnp
import numpy as np
from jax import lax
from jax.experimental import pallas as pl
from jax.experimental.pallas import tpu as pltpu
from jax.sharding import PartitionSpec as P

delta_abs = 0.1
both_axes = ("lat", "ens")


def wave_table(mode_count, lon_count):
    points = np.arange(lon_count, dtype=np.int64)
    modes = np.arange(mode_count, dtype=np.int64)
    phase = modes[:, None] * points[None, :] % lon_count
    angle = phase.astype(np.float32) * np.float32(2.0 * math.pi / lon_count)
    both = np.stack([np.cos(angle), -np.sin(angle)]) / np.float32(math.sqrt(lon_count))
    return both.astype(np.float32).astype(jnp.bfloat16)


def dot(left, right):
    return jnp.dot(left, right, preferred_element_type=jnp.float32)


def flag(condition):
    return jnp.where(condition, 1.0, 0.0).astype(jnp.bfloat16)


def iota(shape, axis):
    return lax.broadcasted_iota(jnp.int32, shape, axis)


def send_kernel(
    place_ref, owner_ref, grid_hbm, waves_hbm, legendre_hbm, out_ref, codes_ref,
    grid_ref, waves_ref, bands_ref, table_ref, four_ref, mix_ref, sems,
):
    grid_copy = pltpu.make_async_copy(grid_hbm, grid_ref, sems.at[0])
    band_copy = pltpu.make_async_copy(
        legendre_hbm.at[pl.ds(2 * place_ref[0], 2)], bands_ref, sems.at[1]
    )
    wave_copies = [
        pltpu.make_async_copy(
            waves_hbm.at[pl.ds(384 * c, 384)], waves_ref.at[pl.ds(384 * c, 384)], sems.at[2 + c]
        )
        for c in range(2)
    ]
    band_copy.start()
    grid_copy.start()
    for copy in wave_copies:
        copy.start()

    line = jnp.broadcast_to(owner_ref[...].astype(jnp.float32), (128, 384))
    column = jnp.transpose(line, (1, 0))
    lane = iota((384, 128), 1).astype(jnp.float32)
    held = jnp.concatenate([flag(column == lane + 128.0 * t) for t in range(3)], axis=1)
    group = flag(iota((16, 384), 1) // 24 == iota((16, 384), 0))
    lat_of = dot(group, held)
    before = flag(iota((384, 384), 0) < iota((384, 384), 1))
    count = dot(lat_of.astype(jnp.bfloat16), before)
    rank = jnp.sum(lat_of * count, axis=0, keepdims=True)
    lat = jnp.sum(lat_of * iota((16, 384), 0).astype(jnp.float32), axis=0, keepdims=True)
    full_code = jnp.where(rank < 16.0, lat * 16.0 + rank, -1.0)
    half_code = jnp.where(rank >= 16.0, lat * 8.0 + (23.0 - rank), -1.0)
    codes_ref[0:1, :] = full_code
    codes_ref[1:2, :] = half_code
    codes_ref[2:8, :] = jnp.zeros((6, 384), jnp.float32)
    full, even, odd, half = picks(full_code, half_code)

    both = jnp.concatenate([full, half], axis=1)
    band_copy.wait()
    for r in range(2):
        rows = bands_ref[r]
        table_ref[0:384, 0:384] = rows
        table_ref[0:384, 384:512] = jnp.zeros((384, 128), jnp.bfloat16)
        wide = jnp.concatenate([rows.astype(jnp.float32), jnp.zeros((384, 128), jnp.float32)], axis=1)
        for shift in range(1, 13):
            low = max(368 - 32 * shift, 0)
            high = 400 - 32 * shift
            if shift == 1:
                high = 384
                table_ref[384 + 368:768, :] = wide[368:384].astype(jnp.bfloat16)
                high = 368
            moved = pltpu.roll(wide[low:high], 32 * shift, 1)
            table_ref[384 + low:384 + high, :] = moved.astype(jnp.bfloat16)
        packed = dot(both, table_ref[...])
        for t in range(4):
            mix_ref[3 + t, pl.ds(r, 256, stride=2), :] = packed[:, 128 * t:128 * t + 128]

    grid_copy.wait()
    for c in range(2):
        wave_copies[c].wait()
        four_ref[384 * c:384 * c + 384, :] = lax.dot_general(
            waves_ref[384 * c:384 * c + 384, :], grid_ref[...], (((1,), (1,)), ((), ())),
            preferred_element_type=jnp.float32,
        ).astype(jnp.bfloat16)
        part = dot(full, four_ref[384 * c:384 * c + 384, :])
        for h in range(2):
            mix_ref[h, pl.ds(c, 256, stride=2), :] = part[:, 128 * h:128 * h + 128]
    part = dot(jnp.concatenate([even, odd], axis=1), four_ref[...])
    for h in range(2):
        mix_ref[2, pl.ds(h, 256, stride=2), :] = part[:, 128 * h:128 * h + 128]
    for t in range(7):
        out_ref[:, 128 * t:128 * t + 128] = mix_ref[t].astype(jnp.bfloat16)


def picks(full_code, half_code):
    row = iota((256, 384), 0)
    full = flag(row.astype(jnp.float32) == full_code)
    match = (row // 2).astype(jnp.float32) == half_code
    even = flag(match & (row % 2 == 0))
    odd = flag(match & (row % 2 == 1))
    return full, even, odd, flag(match)


def send_call(place, owner, grid, waves, legendre):
    vmem = pl.BlockSpec(memory_space=pltpu.VMEM)
    anywhere = pl.BlockSpec(memory_space=pltpu.HBM)
    return pl.pallas_call(
        send_kernel,
        out_shape=(
            jax.ShapeDtypeStruct((512, 896), jnp.bfloat16),
            jax.ShapeDtypeStruct((8, 384), jnp.float32),
        ),
        in_specs=[pl.BlockSpec(memory_space=pltpu.SMEM), vmem, anywhere, anywhere, anywhere],
        out_specs=(vmem, vmem),
        scratch_shapes=[
            pltpu.VMEM((256, 1440), jnp.bfloat16),
            pltpu.VMEM((768, 1440), jnp.bfloat16),
            pltpu.VMEM((2, 384, 384), jnp.bfloat16),
            pltpu.VMEM((768, 512), jnp.bfloat16),
            pltpu.VMEM((768, 256), jnp.bfloat16),
            pltpu.VMEM((7, 512, 128), jnp.float32),
            pltpu.SemaphoreType.DMA((4,)),
        ],
        compiler_params=pltpu.CompilerParams(vmem_limit_bytes=20 * 1024 * 1024),
    )(place, owner, grid, waves, legendre)


def score_kernel(
    orders_ref, got_ref, full_ref, half_ref, cutoff_ref, back_ref,
    rows_ref, tiled_ref, coeffs_ref, grads_ref, wide_ref,
):
    lane_field = iota((32, 128), 1) // 32
    for j in range(16):
        for q in range(3):
            block = got_ref[32 * j:32 * j + 32, 128 * q:128 * q + 128]
            for k in range(4):
                row = (q * 4 + k) * 32
                rows_ref[row:row + 32, 128 * j:128 * j + 128] = jnp.where(
                    lane_field == k, block, jnp.zeros_like(block)
                )
        band = got_ref[32 * j:32 * j + 32, 384:896]
        for k in range(4):
            tiled_ref[128 * j + 32 * k:128 * j + 32 * k + 32, :] = band
    coeffs = dot(rows_ref[...], tiled_ref[...])
    for t in range(4):
        coeffs_ref[t] = coeffs[:, 128 * t:128 * t + 128]
    offset = delta_abs * delta_abs
    limit = cutoff_ref[...]

    def column(level, order, goal, load, store):
        inside = (level >= order) & (level <= limit)
        member = [load(e) for e in range(16)]
        slope = [jnp.zeros((8, 128), jnp.float32) for _ in range(16)]
        pair_value = jnp.zeros((8, 128), jnp.float32)
        for i in range(16):
            for k in range(i + 1, 16):
                spread = member[i] - member[k]
                square = spread * spread + offset
                inverse = lax.rsqrt(square)
                step_slope = spread * inverse
                slope[i] = slope[i] + step_slope
                slope[k] = slope[k] - step_slope
                pair_value = pair_value + (square * inverse - delta_abs)
        own_value = jnp.zeros((8, 128), jnp.float32)
        for i in range(16):
            spread = member[i] - goal
            square = spread * spread + offset
            inverse = lax.rsqrt(square)
            own_value = own_value + (square * inverse - delta_abs)
            store(i, jnp.where(inside, spread * inverse - slope[i] / 16.0, 0.0))
        return jnp.where(inside, own_value / 16.0 - pair_value / 256.0, 0.0)

    def full_column(step, total):
        part = step // 3
        third = step % 3
        lanes = pl.ds(pl.multiple_of(third * 128, 128), 128)

        def load(e):
            return coeffs_ref[third, pl.ds(2 * e + part, 8, stride=32), :]

        def store(e, value):
            grads_ref[pl.ds(pl.multiple_of(part * 128 + 8 * e, 8), 8), lanes] = value

        goal = full_ref[pl.ds(pl.multiple_of(part * 8, 8), 8), lanes]
        return total + column(iota((8, 128), 1) + third * 128, orders_ref[0], goal, load, store)

    def half_column(tile, total):
        lanes = pl.ds(pl.multiple_of(tile * 128, 128), 128)

        def load(e):
            return jnp.concatenate(
                [coeffs_ref[tile, pl.ds(256 + 2 * e + h, 4, stride=32), :] for h in range(2)]
            )

        def store(e, value):
            grads_ref[256 + 8 * e:256 + 8 * e + 8, lanes] = value

        level = iota((8, 128), 1) + tile * 128 - orders_ref[2]
        level = jnp.where(level < 0, level + 512, level)
        return total + column(level, orders_ref[1], half_ref[:, lanes], load, store)

    total = lax.fori_loop(0, 6, full_column, jnp.zeros((8, 128), jnp.float32))
    total = lax.fori_loop(0, 4, half_column, total)
    grads_ref[0:256, 384:512] = jnp.zeros((256, 128), jnp.float32)
    score = jnp.sum(jnp.sum(total, axis=1, keepdims=True), axis=0, keepdims=True)
    high = score.astype(jnp.bfloat16).astype(jnp.float32)
    middle = (score - high).astype(jnp.bfloat16).astype(jnp.float32)
    low = score - high - middle
    spot = iota((128, 128), 1)
    pieces = jnp.where(spot == 96, high, jnp.where(spot == 97, middle, jnp.where(spot == 98, low, 0.0)))

    wide_ref[...] = lax.dot_general(
        grads_ref[...].astype(jnp.bfloat16), tiled_ref[...], (((1,), (1,)), ((), ())),
        preferred_element_type=jnp.float32,
    )
    for j in range(16):
        lanes = slice(128 * j, 128 * j + 128)
        merged = jnp.where(
            spot < 32, wide_ref[0:128, lanes],
            jnp.where(spot < 64, wide_ref[128:256, lanes], jnp.where(spot < 96, wide_ref[256:384, lanes], pieces)),
        )
        back_ref[128 * j:128 * j + 128, :] = merged.astype(jnp.bfloat16)


def score_call(orders, got, full_rows, half_rows, limit):
    vmem = pl.BlockSpec(memory_space=pltpu.VMEM)
    return pl.pallas_call(
        score_kernel,
        out_shape=jax.ShapeDtypeStruct((2048, 128), jnp.bfloat16),
        in_specs=[pl.BlockSpec(memory_space=pltpu.SMEM), vmem, vmem, vmem, vmem],
        out_specs=vmem,
        scratch_shapes=[
            pltpu.VMEM((384, 2048), jnp.bfloat16),
            pltpu.VMEM((2048, 512), jnp.bfloat16),
            pltpu.VMEM((4, 384, 128), jnp.float32),
            pltpu.VMEM((384, 512), jnp.float32),
            pltpu.VMEM((384, 2048), jnp.float32),
        ],
        compiler_params=pltpu.CompilerParams(vmem_limit_bytes=20 * 1024 * 1024),
    )(orders, got, full_rows, half_rows, limit)


def home_kernel(valid_ref, codes_ref, got_ref, waves_ref, score_ref, out_ref, mix_ref, turned_ref):
    mix_ref[...] = got_ref[...].astype(jnp.float32)
    for f in range(8):
        rows = mix_ref[pl.ds(f, 256, stride=8), :]
        if f == 0:
            spot = iota((256, 128), 1)
            pieces = jnp.where((spot >= 96) & (spot < 99), rows, 0.0)
            score_ref[0] = jnp.sum(pieces) / valid_ref[0]
        turned = jnp.transpose(rows, (1, 0)).astype(jnp.bfloat16)
        for w in range(3):
            turned_ref[w, 32 * f:32 * f + 32, :] = turned[32 * w:32 * w + 32]
    full, even, odd, _ = picks(codes_ref[0:1, :], codes_ref[1:2, :])
    first = dot(turned_ref[0], full) + dot(turned_ref[2], even)
    second = dot(turned_ref[1], full) + dot(turned_ref[2], odd)
    natural = jnp.concatenate([first, second], axis=1).astype(jnp.bfloat16)
    out_ref[...] = dot(natural, waves_ref[...]).astype(jnp.bfloat16)


def home_call(valid, codes, got, waves):
    vmem = pl.BlockSpec(memory_space=pltpu.VMEM)
    smem = pl.BlockSpec(memory_space=pltpu.SMEM)
    return pl.pallas_call(
        home_kernel,
        out_shape=(
            jax.ShapeDtypeStruct((1,), jnp.float32),
            jax.ShapeDtypeStruct((256, waves.shape[1]), jnp.bfloat16),
        ),
        in_specs=[smem, vmem, vmem, vmem],
        out_specs=(smem, vmem),
        scratch_shapes=[pltpu.VMEM((2048, 128), jnp.float32), pltpu.VMEM((3, 256, 256), jnp.bfloat16)],
        compiler_params=pltpu.CompilerParams(vmem_limit_bytes=20 * 1024 * 1024),
    )(valid, codes, got, waves)


def exchange(rows):
    return lax.all_to_all(rows, both_axes, split_axis=0, concat_axis=0, tiled=True)


def shift_of(order):
    return jnp.where(order >= 368, 0, (368 - order + 31) // 32 * 32)


def ranked(orders):
    rank = jnp.sum((orders[..., None] > orders[..., None, :]).astype(jnp.int32), axis=-1)
    return rank


def exact(equation, left, right):
    return jnp.einsum(equation, left, right, preferred_element_type=jnp.float32).astype(jnp.bfloat16)


def unpacked(grid, legendre, target, owner, cutoff, waves, modes_valid):
    fields, rows = grid.shape[1:3]
    modes, levels = legendre.shape[1:]
    e = lax.axis_index("ens")
    j = lax.axis_index("lat")
    natural = jnp.arange(modes, dtype=jnp.int32)
    place = jnp.arange(256, dtype=jnp.int32)
    full_slots = place // 16 * 24 + place % 16
    half_slots = place // 16 * 24 + 16 + place % 16 // 2
    pick_full = (owner[full_slots][:, None] == natural).astype(jnp.bfloat16)
    pick_half = (owner[half_slots][:, None] == natural).astype(jnp.bfloat16)
    zeros = jnp.zeros_like(pick_full)
    odd = (place % 2 == 1)[:, None]
    pick = jnp.stack([
        jnp.stack([pick_full, zeros], axis=1),
        jnp.stack([zeros, pick_full], axis=1),
        jnp.stack([jnp.where(odd, zeros, pick_half), jnp.where(odd, pick_half, zeros)], axis=1),
    ], axis=1)
    table = waves.reshape(2, modes, -1)
    fourier = exact("cmn,fan->cmfa", table, grid[0])
    fourier = exchange(exact("dwcm,cmfa->dwfa", pick, fourier).reshape(256, 6, 128))
    fourier = fourier.reshape(16, 16, 3, fields, rows)
    bands = lax.dynamic_slice_in_dim(legendre, 2 * e, 2, axis=0)
    pick_orders = jnp.stack([pick_full, pick_half], axis=1)
    weights = exchange(exact("dom,rml->drol", pick_orders, bands).reshape(256, 4, levels))
    weights = weights.reshape(16, rows, 2, levels)
    weights = jnp.stack([weights[:, :, 0], weights[:, :, 0], weights[:, :, 1]], axis=2)
    coeffs = jnp.einsum("jewfa,jawl->ewfl", fourier, weights, preferred_element_type=jnp.float32)

    own = lax.dynamic_slice_in_dim(owner, 24 * j, 24)
    full_rows = lax.dynamic_index_in_dim(target, e, 0, keepdims=False)
    half_rows = lax.dynamic_slice(target, (16 + e // 2, 0, e % 2, 0), (1, fields, 1, levels))[0, :, 0]
    goal = jnp.stack([full_rows[:, 0], full_rows[:, 1], half_rows])
    order = jnp.stack([own[e], own[e], own[16 + e // 2]])[:, None, None]
    level = jnp.arange(levels, dtype=jnp.int32)
    inside = ((level >= order) & (level <= cutoff[None, :, None])).astype(jnp.float32)
    offset = delta_abs * delta_abs
    spread = coeffs[:, None] - coeffs[None]
    height = jnp.sqrt(spread * spread + offset)
    pair_value = jnp.sum(height - delta_abs, axis=1)
    pair_slope = jnp.sum(spread / height, axis=1)
    spread = coeffs - goal
    height = jnp.sqrt(spread * spread + offset)
    score = jnp.sum(inside * ((height - delta_abs) / 16.0 - pair_value / 512.0))
    grad = (inside * (spread / height - pair_slope / 16.0)).astype(jnp.bfloat16)
    score = exchange(jnp.full((256, 1, 128), score, jnp.float32))
    mean_score = (jnp.sum(score[:, 0, 0]) / modes_valid[0]).reshape(1)

    back = exchange(exact("ewfl,jawl->jewfa", grad, weights).reshape(256, 6, 128))
    back = exact("dwcm,dwfa->facm", pick, back.reshape(256, 3, fields, rows))
    return mean_score, exact("facm,cmn->fan", back, table)[None]


def body(grid, legendre, target, owner, cutoff):
    fields, rows, lon_count = grid.shape[1:]
    modes = legendre.shape[1]
    e = lax.axis_index("ens")
    j = lax.axis_index("lat")
    waves = jnp.asarray(wave_table(modes, lon_count).reshape(2 * modes, lon_count))
    sent, codes = send_call(
        e.reshape(1), owner.reshape(1, modes), grid.reshape(fields * rows, lon_count), waves, legendre
    )
    got = exchange(sent.reshape(256, 2, 896)).reshape(512, 896)

    by_lat = owner.reshape(16, 24)
    rank = ranked(by_lat)
    spots = jnp.arange(24, dtype=jnp.int32)
    by_rank = jnp.sum(jnp.where(rank[:, :, None] == spots, by_lat[:, :, None], 0), axis=1)
    long_orders = by_rank[:, 0:16:2]
    short_orders = by_rank[:, 23:15:-1]
    fits = jnp.all(360 + shift_of(short_orders) <= 511 + long_orders)

    own = lax.dynamic_slice_in_dim(owner, 24 * j, 24)
    own_rank = ranked(own)
    is_full = own_rank == e
    is_half = own_rank == 23 - e // 2
    full_order = jnp.sum(jnp.where(is_full, own, 0))
    half_order = jnp.sum(jnp.where(is_half, own, 0))
    shift = shift_of(half_order)
    orders = jnp.stack([full_order, half_order, shift])
    full_slot = jnp.sum(jnp.where(is_full, spots, 0))
    half_slot = jnp.sum(jnp.where(is_half, spots, 0))
    full_rows = lax.dynamic_index_in_dim(target, full_slot, 0, keepdims=False)
    full_rows = jnp.concatenate([full_rows[:, 0], full_rows[:, 1]])
    half_rows = lax.dynamic_slice(target, (half_slot, 0, e % 2, 0), (1, fields, 1, target.shape[3]))
    half_rows = jnp.pad(half_rows[0, :, 0], ((0, 0), (0, 512 - target.shape[3])))
    half_rows = lax.dynamic_slice_in_dim(jnp.concatenate([half_rows, half_rows], axis=1), 512 - shift, 512, axis=1)
    limit = jnp.broadcast_to(cutoff[:, None], (fields, 128))
    cut_level = cutoff.astype(jnp.float32)
    modes_valid = jnp.sum((cut_level + 1.0) * (cut_level + 2.0)).reshape(1)

    back = score_call(orders, got, full_rows, half_rows, limit)
    home = exchange(back.reshape(256, 8, 128)).reshape(2048, 128)
    mean_score, grid_grad = home_call(modes_valid, codes, home, waves)
    grid_grad = grid_grad.reshape(1, fields, rows, lon_count)
    return lax.cond(
        fits,
        lambda: (mean_score, grid_grad),
        lambda: unpacked(grid, legendre, target, owner, cutoff, waves, modes_valid),
    )


def solution(mesh):
    in_specs = (
        P("ens", None, "lat", None),
        P("lat", None, None),
        P("lat", None, None, None),
        P(),
        P(),
    )
    out_specs = (P(), P("ens", None, "lat", None))
    return jax.shard_map(body, mesh=mesh, in_specs=in_specs, out_specs=out_specs, check_vma=False)
```

```python
import math

import jax
import jax.numpy as jnp
import numpy as np
from jax import lax
from jax.experimental import pallas as pl
from jax.experimental.pallas import tpu as pltpu
from jax.sharding import PartitionSpec as P

delta_abs = 0.1
both_axes = ("lat", "ens")


def wave_table(mode_count, lon_count):
    points = np.arange(lon_count, dtype=np.int64)
    modes = np.arange(mode_count, dtype=np.int64)
    phase = modes[:, None] * points[None, :] % lon_count
    angle = phase.astype(np.float32) * np.float32(2.0 * math.pi / lon_count)
    both = np.stack([np.cos(angle), -np.sin(angle)]) / np.float32(math.sqrt(lon_count))
    return both.astype(np.float32).astype(jnp.bfloat16)


def dot(left, right):
    return jnp.dot(left, right, preferred_element_type=jnp.float32)


def flag(condition):
    return jnp.where(condition, 1.0, 0.0).astype(jnp.bfloat16)


def iota(shape, axis):
    return lax.broadcasted_iota(jnp.int32, shape, axis)


def send_kernel(
    place_ref, owner_hbm, grid_hbm, waves_hbm, legendre_hbm, out_ref, codes_ref,
    owner_ref, grid_ref, waves_ref, bands_ref, table_ref, four_ref, mix_ref, sems,
):
    grid_copy = pltpu.make_async_copy(grid_hbm, grid_ref, sems.at[0])
    band_copy = pltpu.make_async_copy(
        legendre_hbm.at[pl.ds(2 * place_ref[0], 2)], bands_ref, sems.at[1]
    )
    wave_copies = [
        pltpu.make_async_copy(
            waves_hbm.at[:, pl.ds(384 * c, 384)], waves_ref.at[:, pl.ds(384 * c, 384)], sems.at[2 + c]
        )
        for c in range(2)
    ]
    owner_copy = pltpu.make_async_copy(owner_hbm, owner_ref, sems.at[4])
    owner_copy.start()
    band_copy.start()
    grid_copy.start()
    for copy in wave_copies:
        copy.start()

    owner_copy.wait()
    line = jnp.broadcast_to(owner_ref[...].reshape(1, 384).astype(jnp.float32), (128, 384))
    column = jnp.transpose(line, (1, 0))
    lane = iota((384, 128), 1).astype(jnp.float32)
    held = jnp.concatenate([flag(column == lane + 128.0 * t) for t in range(3)], axis=1)
    group = flag(iota((16, 384), 1) // 24 == iota((16, 384), 0))
    lat_of = dot(group, held)
    before = flag(iota((384, 384), 0) < iota((384, 384), 1))
    count = dot(lat_of.astype(jnp.bfloat16), before)
    rank = jnp.sum(lat_of * count, axis=0, keepdims=True)
    lat = jnp.sum(lat_of * iota((16, 384), 0).astype(jnp.float32), axis=0, keepdims=True)
    full_code = jnp.where(rank < 16.0, lat * 16.0 + rank, -1.0)
    half_code = jnp.where(rank >= 16.0, lat * 8.0 + (23.0 - rank), -1.0)
    codes_ref[0:1, :] = full_code
    codes_ref[1:2, :] = half_code
    codes_ref[2:8, :] = jnp.zeros((6, 384), jnp.float32)
    full, even, odd, half = picks(full_code, half_code)

    both = jnp.concatenate([full, half], axis=1)
    band_copy.wait()
    for r in range(2):
        rows = bands_ref[r]
        table_ref[0:384, 0:384] = rows
        table_ref[0:384, 384:512] = jnp.zeros((384, 128), jnp.bfloat16)
        wide = jnp.concatenate([rows.astype(jnp.float32), jnp.zeros((384, 128), jnp.float32)], axis=1)
        for shift in range(1, 13):
            low = max(368 - 32 * shift, 0)
            high = 400 - 32 * shift
            if shift == 1:
                high = 384
                table_ref[384 + 368:768, :] = wide[368:384].astype(jnp.bfloat16)
                high = 368
            moved = pltpu.roll(wide[low:high], 32 * shift, 1)
            table_ref[384 + low:384 + high, :] = moved.astype(jnp.bfloat16)
        packed = dot(both, table_ref[...])
        for t in range(4):
            mix_ref[3 + t, pl.ds(r, 256, stride=2), :] = packed[:, 128 * t:128 * t + 128]

    for t in range(3, 7):
        out_ref[:, :, 128 * t:128 * t + 128] = mix_ref[t].astype(jnp.bfloat16).reshape(256, 2, 128)

    dims = (((1,), (1,)), ((), ()))
    grid_copy.wait()
    for c in range(2):
        wave_copies[c].wait()
        columns = slice(384 * c, 384 * c + 384)
        four_ref[:, columns] = dot(grid_ref[...], waves_ref[:, columns]).astype(jnp.bfloat16)
        part = lax.dot_general(full, four_ref[:, columns], dims, preferred_element_type=jnp.float32)
        for h in range(2):
            mix_ref[h, pl.ds(c, 256, stride=2), :] = part[:, 128 * h:128 * h + 128]
    part = lax.dot_general(
        jnp.concatenate([even, odd], axis=1), four_ref[...], dims, preferred_element_type=jnp.float32
    )
    for h in range(2):
        mix_ref[2, pl.ds(h, 256, stride=2), :] = part[:, 128 * h:128 * h + 128]
    for t in range(3):
        out_ref[:, :, 128 * t:128 * t + 128] = mix_ref[t].astype(jnp.bfloat16).reshape(256, 2, 128)


def picks(full_code, half_code):
    row = iota((256, 384), 0)
    full = flag(row.astype(jnp.float32) == full_code)
    match = (row // 2).astype(jnp.float32) == half_code
    even = flag(match & (row % 2 == 0))
    odd = flag(match & (row % 2 == 1))
    return full, even, odd, flag(match)


def send_call(place, owner, grid, waves, legendre):
    vmem = pl.BlockSpec(memory_space=pltpu.VMEM)
    anywhere = pl.BlockSpec(memory_space=pltpu.HBM)
    return pl.pallas_call(
        send_kernel,
        out_shape=(
            jax.ShapeDtypeStruct((256, 2, 896), jnp.bfloat16),
            jax.ShapeDtypeStruct((8, 384), jnp.float32),
        ),
        in_specs=[pl.BlockSpec(memory_space=pltpu.SMEM), anywhere, anywhere, anywhere, anywhere],
        out_specs=(vmem, vmem),
        scratch_shapes=[
            pltpu.VMEM((384,), jnp.int32),
            pltpu.VMEM((256, 1440), jnp.bfloat16),
            pltpu.VMEM((1440, 768), jnp.bfloat16),
            pltpu.VMEM((2, 384, 384), jnp.bfloat16),
            pltpu.VMEM((768, 512), jnp.bfloat16),
            pltpu.VMEM((256, 768), jnp.bfloat16),
            pltpu.VMEM((7, 512, 128), jnp.float32),
            pltpu.SemaphoreType.DMA((5,)),
        ],
        compiler_params=pltpu.CompilerParams(vmem_limit_bytes=58 * 1024 * 1024),
    )(place, owner, grid, waves, legendre)


def score_kernel(
    orders_ref, got_ref, full_ref, half_ref, cutoff_ref, back_ref,
    flat_ref, rows_ref, coeffs_ref, grads_ref, total_ref,
):
    flat_ref[...] = got_ref[...].reshape(512, 896)
    lane_group = iota((32, 128), 1) // 32
    for q in range(3):
        for group in range(4):
            blocks = [
                flat_ref[128 * group + 32 * i:128 * group + 32 * i + 32, 128 * q:128 * q + 128].astype(jnp.float32)
                for i in range(4)
            ]
            for k in range(4):
                merged = jnp.zeros((32, 128), jnp.float32)
                for i in range(4):
                    turn = (i - k) % 4
                    block = pltpu.roll(blocks[i], 32 * turn, 1) if turn else blocks[i]
                    merged = jnp.where(lane_group == i, block, merged)
                row = (q * 4 + k) * 32
                rows_ref[row:row + 32, 128 * group:128 * group + 128] = merged.astype(jnp.bfloat16)
    coeffs = dot(rows_ref[...], flat_ref[:, 384:896])
    for t in range(4):
        coeffs_ref[t] = coeffs[:, 128 * t:128 * t + 128]
    offset = delta_abs * delta_abs
    limit = cutoff_ref[...]

    def column(level, order, goal, load, store):
        inside = (level >= order) & (level <= limit)
        member = [load(e) for e in range(16)]
        slope = [jnp.zeros((8, 128), jnp.float32) for _ in range(16)]
        rest = jnp.zeros((8, 128), jnp.float32)
        for i in range(16):
            for k in range(i + 1, 16):
                spread = member[i] - member[k]
                inverse = lax.rsqrt(spread * spread + offset)
                step_slope = spread * inverse
                slope[i] = slope[i] + step_slope
                slope[k] = slope[k] - step_slope
                rest = rest + (inverse - 1.0 / delta_abs)
        pair_value = offset * rest
        for i in range(1, 16):
            pair_value = pair_value + (member[i] - member[0]) * slope[i]
        own_value = jnp.zeros((8, 128), jnp.float32)
        for i in range(16):
            spread = member[i] - goal
            square = spread * spread + offset
            inverse = lax.rsqrt(square)
            own_value = own_value + (square * inverse - delta_abs)
            store(i, jnp.where(inside, spread * inverse - slope[i] / 16.0, 0.0))
        total_ref[...] += jnp.where(inside, own_value / 16.0 - pair_value / 256.0, 0.0)

    total_ref[...] = jnp.zeros((8, 128), jnp.float32)
    full_order, half_order, shift, highest = [orders_ref[i] for i in range(4)]

    @pl.loop(0, 6)
    def _(step):
        part = step // 3
        third = step % 3
        lanes = pl.ds(pl.multiple_of(third * 128, 128), 128)
        first = third * 128
        active = (first + 127 >= full_order) & (first <= highest)

        def load(e):
            return coeffs_ref[third, pl.ds(2 * e + part, 8, stride=32), :]

        def store(e, value):
            grads_ref[pl.ds(pl.multiple_of(part * 128 + 8 * e, 8), 8), lanes] = value

        @pl.when(active)
        def _():
            goal = full_ref[pl.ds(pl.multiple_of(part * 8, 8), 8), lanes]
            column(iota((8, 128), 1) + first, full_order, goal, load, store)

        @pl.when(jnp.logical_not(active))
        def _():
            grads_ref[pl.ds(pl.multiple_of(part * 128, 128), 128), lanes] = jnp.zeros((128, 128), jnp.float32)

    @pl.loop(0, 4)
    def _(tile):
        lanes = pl.ds(pl.multiple_of(tile * 128, 128), 128)
        first = tile * 128 - shift
        first = jnp.where(first < 0, first + 512, first)
        active = ((first + 127 >= half_order) & (first <= highest)) | (first - 385 >= half_order)

        def load(e):
            return jnp.concatenate(
                [coeffs_ref[tile, pl.ds(256 + 2 * e + h, 4, stride=32), :] for h in range(2)]
            )

        def store(e, value):
            grads_ref[256 + 8 * e:256 + 8 * e + 8, lanes] = value

        @pl.when(active)
        def _():
            level = iota((8, 128), 1) + first
            level = jnp.where(level >= 512, level - 512, level)
            column(level, half_order, half_ref[:, lanes], load, store)

        @pl.when(jnp.logical_not(active))
        def _():
            grads_ref[256:384, lanes] = jnp.zeros((128, 128), jnp.float32)

    grads_ref[0:256, 384:512] = jnp.zeros((256, 128), jnp.float32)
    total = total_ref[...]
    score = jnp.sum(jnp.sum(total, axis=1, keepdims=True), axis=0, keepdims=True)
    high = score.astype(jnp.bfloat16).astype(jnp.float32)
    middle = (score - high).astype(jnp.bfloat16).astype(jnp.float32)
    low = score - high - middle
    spot = iota((128, 128), 1)
    pieces = jnp.where(spot == 96, high, jnp.where(spot == 97, middle, jnp.where(spot == 98, low, 0.0)))

    waves_grad = lax.dot_general(
        grads_ref[...].astype(jnp.bfloat16), flat_ref[:, 384:896], (((1,), (1,)), ((), ())),
        preferred_element_type=jnp.float32,
    )
    for j in range(16):
        merged = pieces
        for w in range(3):
            block = waves_grad[128 * w:128 * w + 128, 128 * (j // 4):128 * (j // 4) + 128]
            turn = (w - j) % 4
            if turn:
                block = pltpu.roll(block, 32 * turn, 1)
            merged = jnp.where(spot // 32 == w, block, merged)
        back_ref[128 * j:128 * j + 128, :] = merged.astype(jnp.bfloat16)


def score_call(orders, got, full_rows, half_rows, limit):
    vmem = pl.BlockSpec(memory_space=pltpu.VMEM)
    return pl.pallas_call(
        score_kernel,
        out_shape=jax.ShapeDtypeStruct((2048, 128), jnp.bfloat16),
        in_specs=[pl.BlockSpec(memory_space=pltpu.SMEM), vmem, vmem, vmem, vmem],
        out_specs=vmem,
        scratch_shapes=[
            pltpu.VMEM((512, 896), jnp.bfloat16),
            pltpu.VMEM((384, 512), jnp.bfloat16),
            pltpu.VMEM((4, 384, 128), jnp.float32),
            pltpu.VMEM((384, 512), jnp.float32),
            pltpu.VMEM((8, 128), jnp.float32),
        ],
        compiler_params=pltpu.CompilerParams(vmem_limit_bytes=20 * 1024 * 1024),
    )(orders, got, full_rows, half_rows, limit)


def home_kernel(valid_ref, codes_ref, got_ref, waves_ref, score_ref, out_ref, mix_ref, turned_ref):
    mix_ref[...] = got_ref[...].astype(jnp.float32)
    for f in range(8):
        rows = mix_ref[pl.ds(f, 256, stride=8), :]
        if f == 0:
            spot = iota((256, 128), 1)
            pieces = jnp.where((spot >= 96) & (spot < 99), rows, 0.0)
            score_ref[0] = jnp.sum(pieces) / valid_ref[0]
        turned = jnp.transpose(rows, (1, 0)).astype(jnp.bfloat16)
        for w in range(3):
            turned_ref[w, 32 * f:32 * f + 32, :] = turned[32 * w:32 * w + 32]
    full, even, odd, _ = picks(codes_ref[0:1, :], codes_ref[1:2, :])
    first = dot(turned_ref[0], full) + dot(turned_ref[2], even)
    second = dot(turned_ref[1], full) + dot(turned_ref[2], odd)
    natural = jnp.concatenate([first, second], axis=1).astype(jnp.bfloat16)
    out_ref[...] = dot(natural, waves_ref[...]).astype(jnp.bfloat16)


def home_call(valid, codes, got, waves):
    vmem = pl.BlockSpec(memory_space=pltpu.VMEM)
    smem = pl.BlockSpec(memory_space=pltpu.SMEM)
    return pl.pallas_call(
        home_kernel,
        out_shape=(
            jax.ShapeDtypeStruct((1,), jnp.float32),
            jax.ShapeDtypeStruct((256, waves.shape[1]), jnp.bfloat16),
        ),
        in_specs=[smem, vmem, vmem, vmem],
        out_specs=(smem, vmem),
        scratch_shapes=[pltpu.VMEM((2048, 128), jnp.float32), pltpu.VMEM((3, 256, 256), jnp.bfloat16)],
        compiler_params=pltpu.CompilerParams(vmem_limit_bytes=20 * 1024 * 1024),
    )(valid, codes, got, waves)


def exchange(rows):
    return lax.all_to_all(rows, both_axes, split_axis=0, concat_axis=0, tiled=True)


def shift_of(order):
    return jnp.where(order >= 368, 0, (368 - order + 31) // 32 * 32)


def ranked(orders):
    rank = jnp.sum((orders[..., None] > orders[..., None, :]).astype(jnp.int32), axis=-1)
    return rank


def exact(equation, left, right):
    return jnp.einsum(equation, left, right, preferred_element_type=jnp.float32).astype(jnp.bfloat16)


def unpacked(grid, legendre, target, owner, cutoff, waves, modes_valid):
    fields, rows = grid.shape[1:3]
    modes, levels = legendre.shape[1:]
    e = lax.axis_index("ens")
    j = lax.axis_index("lat")
    natural = jnp.arange(modes, dtype=jnp.int32)
    place = jnp.arange(256, dtype=jnp.int32)
    full_slots = place // 16 * 24 + place % 16
    half_slots = place // 16 * 24 + 16 + place % 16 // 2
    pick_full = (owner[full_slots][:, None] == natural).astype(jnp.bfloat16)
    pick_half = (owner[half_slots][:, None] == natural).astype(jnp.bfloat16)
    zeros = jnp.zeros_like(pick_full)
    odd = (place % 2 == 1)[:, None]
    pick = jnp.stack([
        jnp.stack([pick_full, zeros], axis=1),
        jnp.stack([zeros, pick_full], axis=1),
        jnp.stack([jnp.where(odd, zeros, pick_half), jnp.where(odd, pick_half, zeros)], axis=1),
    ], axis=1)
    table = waves.reshape(2, modes, -1)
    fourier = exact("cmn,fan->cmfa", table, grid[0])
    fourier = exchange(exact("dwcm,cmfa->dwfa", pick, fourier).reshape(256, 6, 128))
    fourier = fourier.reshape(16, 16, 3, fields, rows)
    bands = lax.dynamic_slice_in_dim(legendre, 2 * e, 2, axis=0)
    pick_orders = jnp.stack([pick_full, pick_half], axis=1)
    weights = exchange(exact("dom,rml->drol", pick_orders, bands).reshape(256, 4, levels))
    weights = weights.reshape(16, rows, 2, levels)
    weights = jnp.stack([weights[:, :, 0], weights[:, :, 0], weights[:, :, 1]], axis=2)
    coeffs = jnp.einsum("jewfa,jawl->ewfl", fourier, weights, preferred_element_type=jnp.float32)

    own = lax.dynamic_slice_in_dim(owner, 24 * j, 24)
    full_rows = lax.dynamic_index_in_dim(target, e, 0, keepdims=False)
    half_rows = lax.dynamic_slice(target, (16 + e // 2, 0, e % 2, 0), (1, fields, 1, levels))[0, :, 0]
    goal = jnp.stack([full_rows[:, 0], full_rows[:, 1], half_rows])
    order = jnp.stack([own[e], own[e], own[16 + e // 2]])[:, None, None]
    level = jnp.arange(levels, dtype=jnp.int32)
    inside = ((level >= order) & (level <= cutoff[None, :, None])).astype(jnp.float32)
    offset = delta_abs * delta_abs
    spread = coeffs[:, None] - coeffs[None]
    height = jnp.sqrt(spread * spread + offset)
    pair_value = jnp.sum(height - delta_abs, axis=1)
    pair_slope = jnp.sum(spread / height, axis=1)
    spread = coeffs - goal
    height = jnp.sqrt(spread * spread + offset)
    score = jnp.sum(inside * ((height - delta_abs) / 16.0 - pair_value / 512.0))
    grad = (inside * (spread / height - pair_slope / 16.0)).astype(jnp.bfloat16)
    score = exchange(jnp.full((256, 1, 128), score, jnp.float32))
    mean_score = (jnp.sum(score[:, 0, 0]) / modes_valid[0]).reshape(1)

    back = exchange(exact("ewfl,jawl->jewfa", grad, weights).reshape(256, 6, 128))
    back = exact("dwcm,dwfa->facm", pick, back.reshape(256, 3, fields, rows))
    return mean_score, exact("facm,cmn->fan", back, table)[None]


def body(grid, legendre, target, owner, cutoff):
    fields, rows, lon_count = grid.shape[1:]
    modes = legendre.shape[1]
    e = lax.axis_index("ens")
    j = lax.axis_index("lat")
    table = wave_table(modes, lon_count).reshape(2 * modes, lon_count)
    waves = jnp.asarray(table)
    turned = jnp.asarray(np.ascontiguousarray(table.T))
    sent, codes = send_call(
        e.reshape(1), owner, grid.reshape(fields * rows, lon_count), turned, legendre
    )
    got = exchange(sent)

    by_lat = owner.reshape(16, 24)
    rank = ranked(by_lat)
    spots = jnp.arange(24, dtype=jnp.int32)
    by_rank = jnp.sum(jnp.where(rank[:, :, None] == spots, by_lat[:, :, None], 0), axis=1)
    long_orders = by_rank[:, 0:16:2]
    short_orders = by_rank[:, 23:15:-1]
    fits = jnp.all(360 + shift_of(short_orders) <= 511 + long_orders)

    own = lax.dynamic_slice_in_dim(owner, 24 * j, 24)
    own_rank = ranked(own)
    is_full = own_rank == e
    is_half = own_rank == 23 - e // 2
    full_order = jnp.sum(jnp.where(is_full, own, 0))
    half_order = jnp.sum(jnp.where(is_half, own, 0))
    shift = shift_of(half_order)
    orders = jnp.stack([full_order, half_order, shift, jnp.max(cutoff)])
    full_slot = jnp.sum(jnp.where(is_full, spots, 0))
    half_slot = jnp.sum(jnp.where(is_half, spots, 0))
    full_rows = lax.dynamic_index_in_dim(target, full_slot, 0, keepdims=False)
    full_rows = jnp.concatenate([full_rows[:, 0], full_rows[:, 1]])
    half_rows = lax.dynamic_slice(target, (half_slot, 0, e % 2, 0), (1, fields, 1, target.shape[3]))
    half_rows = jnp.pad(half_rows[0, :, 0], ((0, 0), (0, 512 - target.shape[3])))
    half_rows = lax.dynamic_slice_in_dim(jnp.concatenate([half_rows, half_rows], axis=1), 512 - shift, 512, axis=1)
    limit = jnp.broadcast_to(cutoff[:, None], (fields, 128))
    cut_level = cutoff.astype(jnp.float32)
    modes_valid = jnp.sum((cut_level + 1.0) * (cut_level + 2.0)).reshape(1)

    back = score_call(orders, got, full_rows, half_rows, limit)
    home = exchange(back.reshape(256, 8, 128)).reshape(2048, 128)
    mean_score, grid_grad = home_call(modes_valid, codes, home, waves)
    grid_grad = grid_grad.reshape(1, fields, rows, lon_count)
    return lax.cond(
        fits,
        lambda: (mean_score, grid_grad),
        lambda: unpacked(grid, legendre, target, owner, cutoff, waves, modes_valid),
    )


def solution(mesh):
    in_specs = (
        P("ens", None, "lat", None),
        P("lat", None, None),
        P("lat", None, None, None),
        P(),
        P(),
    )
    out_specs = (P(), P("ens", None, "lat", None))
    return jax.shard_map(body, mesh=mesh, in_specs=in_specs, out_specs=out_specs, check_vma=False)
```

```python
import math

import jax
import jax.numpy as jnp
import numpy as np
from jax import lax
from jax.experimental import pallas as pl
from jax.experimental.pallas import tpu as pltpu
from jax.sharding import PartitionSpec as P

delta_abs = 0.1
both_axes = ("lat", "ens")


def wave_table(mode_count, lon_count):
    points = np.arange(lon_count, dtype=np.int64)
    modes = np.arange(mode_count, dtype=np.int64)
    phase = modes[:, None] * points[None, :] % lon_count
    angle = phase.astype(np.float32) * np.float32(2.0 * math.pi / lon_count)
    both = np.stack([np.cos(angle), -np.sin(angle)]) / np.float32(math.sqrt(lon_count))
    return both.astype(np.float32).astype(jnp.bfloat16)


def dot(left, right):
    return jnp.dot(left, right, preferred_element_type=jnp.float32)


def flag(condition):
    return jnp.where(condition, 1.0, 0.0).astype(jnp.bfloat16)


def iota(shape, axis):
    return lax.broadcasted_iota(jnp.int32, shape, axis)


def send_kernel(
    place_ref, owner_hbm, grid_hbm, waves_hbm, legendre_hbm, out_ref, codes_ref,
    owner_ref, grid_ref, waves_ref, bands_ref, table_ref, four_ref, mix_ref, sems,
):
    grid_copy = pltpu.make_async_copy(grid_hbm, grid_ref, sems.at[0])
    band_copy = pltpu.make_async_copy(
        legendre_hbm.at[pl.ds(2 * place_ref[0], 2)], bands_ref, sems.at[1]
    )
    wave_copies = [
        pltpu.make_async_copy(
            waves_hbm.at[:, pl.ds(384 * c, 384)], waves_ref.at[:, pl.ds(384 * c, 384)], sems.at[2 + c]
        )
        for c in range(2)
    ]
    owner_copy = pltpu.make_async_copy(owner_hbm, owner_ref, sems.at[4])
    owner_copy.start()
    band_copy.start()
    grid_copy.start()
    for copy in wave_copies:
        copy.start()

    owner_copy.wait()
    line = jnp.broadcast_to(owner_ref[...].reshape(1, 384).astype(jnp.float32), (128, 384))
    column = jnp.transpose(line, (1, 0))
    lane = iota((384, 128), 1).astype(jnp.float32)
    held = jnp.concatenate([flag(column == lane + 128.0 * t) for t in range(3)], axis=1)
    group = flag(iota((16, 384), 1) // 24 == iota((16, 384), 0))
    lat_of = dot(group, held)
    before = flag(iota((384, 384), 0) < iota((384, 384), 1))
    count = dot(lat_of.astype(jnp.bfloat16), before)
    rank = jnp.sum(lat_of * count, axis=0, keepdims=True)
    lat = jnp.sum(lat_of * iota((16, 384), 0).astype(jnp.float32), axis=0, keepdims=True)
    full_code = jnp.where(rank < 16.0, lat * 16.0 + rank, -1.0)
    half_code = jnp.where(rank >= 16.0, lat * 8.0 + (23.0 - rank), -1.0)
    codes_ref[0:1, :] = full_code
    codes_ref[1:2, :] = half_code
    codes_ref[2:8, :] = jnp.zeros((6, 384), jnp.float32)
    full, even, odd, half = picks(full_code, half_code)

    both = jnp.concatenate([full, half], axis=1)
    band_copy.wait()
    for r in range(2):
        rows = bands_ref[r]
        table_ref[0:384, 0:384] = rows
        table_ref[0:384, 384:512] = jnp.zeros((384, 128), jnp.bfloat16)
        wide = jnp.concatenate([rows.astype(jnp.float32), jnp.zeros((384, 128), jnp.float32)], axis=1)
        for shift in range(1, 13):
            low = max(368 - 32 * shift, 0)
            high = 400 - 32 * shift
            if shift == 1:
                high = 384
                table_ref[384 + 368:768, :] = wide[368:384].astype(jnp.bfloat16)
                high = 368
            moved = pltpu.roll(wide[low:high], 32 * shift, 1)
            table_ref[384 + low:384 + high, :] = moved.astype(jnp.bfloat16)
        packed = dot(both, table_ref[...])
        for t in range(4):
            mix_ref[3 + t, pl.ds(r, 256, stride=2), :] = packed[:, 128 * t:128 * t + 128]

    for t in range(3, 7):
        out_ref[:, :, 128 * t:128 * t + 128] = mix_ref[t].astype(jnp.bfloat16).reshape(256, 2, 128)

    dims = (((1,), (1,)), ((), ()))
    grid_copy.wait()
    for c in range(2):
        wave_copies[c].wait()
        columns = slice(384 * c, 384 * c + 384)
        four_ref[:, columns] = dot(grid_ref[...], waves_ref[:, columns]).astype(jnp.bfloat16)
        part = lax.dot_general(full, four_ref[:, columns], dims, preferred_element_type=jnp.float32)
        for h in range(2):
            mix_ref[h, pl.ds(c, 256, stride=2), :] = part[:, 128 * h:128 * h + 128]
    part = lax.dot_general(
        jnp.concatenate([even, odd], axis=1), four_ref[...], dims, preferred_element_type=jnp.float32
    )
    for h in range(2):
        mix_ref[2, pl.ds(h, 256, stride=2), :] = part[:, 128 * h:128 * h + 128]
    for t in range(3):
        out_ref[:, :, 128 * t:128 * t + 128] = mix_ref[t].astype(jnp.bfloat16).reshape(256, 2, 128)


def picks(full_code, half_code):
    row = iota((256, 384), 0)
    full = flag(row.astype(jnp.float32) == full_code)
    match = (row // 2).astype(jnp.float32) == half_code
    even = flag(match & (row % 2 == 0))
    odd = flag(match & (row % 2 == 1))
    return full, even, odd, flag(match)


def send_call(place, owner, grid, waves, legendre):
    vmem = pl.BlockSpec(memory_space=pltpu.VMEM)
    anywhere = pl.BlockSpec(memory_space=pltpu.HBM)
    return pl.pallas_call(
        send_kernel,
        out_shape=(
            jax.ShapeDtypeStruct((256, 2, 896), jnp.bfloat16),
            jax.ShapeDtypeStruct((8, 384), jnp.float32),
        ),
        in_specs=[pl.BlockSpec(memory_space=pltpu.SMEM), anywhere, anywhere, anywhere, anywhere],
        out_specs=(vmem, vmem),
        scratch_shapes=[
            pltpu.VMEM((384,), jnp.int32),
            pltpu.VMEM((256, 1440), jnp.bfloat16),
            pltpu.VMEM((1440, 768), jnp.bfloat16),
            pltpu.VMEM((2, 384, 384), jnp.bfloat16),
            pltpu.VMEM((768, 512), jnp.bfloat16),
            pltpu.VMEM((256, 768), jnp.bfloat16),
            pltpu.VMEM((7, 512, 128), jnp.float32),
            pltpu.SemaphoreType.DMA((5,)),
        ],
        compiler_params=pltpu.CompilerParams(vmem_limit_bytes=58 * 1024 * 1024),
    )(place, owner, grid, waves, legendre)


def score_kernel(
    orders_ref, got_ref, full_ref, half_ref, cutoff_ref, back_ref,
    flat_ref, rows_ref, coeffs_ref, grads_ref, total_ref,
):
    flat_ref[...] = got_ref[...].reshape(512, 896)
    lane_group = iota((32, 128), 1) // 32
    for q in range(3):
        for group in range(4):
            blocks = [
                flat_ref[128 * group + 32 * i:128 * group + 32 * i + 32, 128 * q:128 * q + 128].astype(jnp.float32)
                for i in range(4)
            ]
            for k in range(4):
                merged = jnp.zeros((32, 128), jnp.float32)
                for i in range(4):
                    turn = (i - k) % 4
                    block = pltpu.roll(blocks[i], 32 * turn, 1) if turn else blocks[i]
                    merged = jnp.where(lane_group == i, block, merged)
                row = (q * 4 + k) * 32
                rows_ref[row:row + 32, 128 * group:128 * group + 128] = merged.astype(jnp.bfloat16)
    coeffs = dot(rows_ref[...], flat_ref[:, 384:896])
    for t in range(4):
        coeffs_ref[t] = coeffs[:, 128 * t:128 * t + 128]
    offset = delta_abs * delta_abs
    limit = cutoff_ref[...]

    def column(level, order, goal, load, store):
        inside = (level >= order) & (level <= limit)
        member = [load(e) for e in range(16)]
        slope = [jnp.zeros((8, 128), jnp.float32) for _ in range(16)]
        rest = jnp.zeros((8, 128), jnp.float32)
        for i in range(16):
            for k in range(i + 1, 16):
                spread = member[i] - member[k]
                inverse = lax.rsqrt(spread * spread + offset)
                step_slope = spread * inverse
                slope[i] = slope[i] + step_slope
                slope[k] = slope[k] - step_slope
                rest = rest + (inverse - 1.0 / delta_abs)
        pair_value = offset * rest
        for i in range(1, 16):
            pair_value = pair_value + (member[i] - member[0]) * slope[i]
        own_value = jnp.zeros((8, 128), jnp.float32)
        for i in range(16):
            spread = member[i] - goal
            square = spread * spread + offset
            inverse = lax.rsqrt(square)
            own_value = own_value + (square * inverse - delta_abs)
            store(i, jnp.where(inside, spread * inverse - slope[i] / 16.0, 0.0))
        total_ref[...] += jnp.where(inside, own_value / 16.0 - pair_value / 256.0, 0.0)

    total_ref[...] = jnp.zeros((8, 128), jnp.float32)
    full_order, half_order, shift, highest = [orders_ref[i] for i in range(4)]

    @pl.loop(0, 6)
    def _(step):
        part = step // 3
        third = step % 3
        lanes = pl.ds(pl.multiple_of(third * 128, 128), 128)
        first = third * 128
        active = (first + 127 >= full_order) & (first <= highest)

        def load(e):
            return coeffs_ref[third, pl.ds(2 * e + part, 8, stride=32), :]

        def store(e, value):
            grads_ref[pl.ds(pl.multiple_of(part * 128 + 8 * e, 8), 8), lanes] = value

        @pl.when(active)
        def _():
            goal = full_ref[pl.ds(pl.multiple_of(part * 8, 8), 8), lanes]
            column(iota((8, 128), 1) + first, full_order, goal, load, store)

        @pl.when(jnp.logical_not(active))
        def _():
            grads_ref[pl.ds(pl.multiple_of(part * 128, 128), 128), lanes] = jnp.zeros((128, 128), jnp.float32)

    @pl.loop(0, 4)
    def _(tile):
        lanes = pl.ds(pl.multiple_of(tile * 128, 128), 128)
        first = tile * 128 - shift
        first = jnp.where(first < 0, first + 512, first)
        active = ((first + 127 >= half_order) & (first <= highest)) | (first - 385 >= half_order)

        def load(e):
            return jnp.concatenate(
                [coeffs_ref[tile, pl.ds(256 + 2 * e + h, 4, stride=32), :] for h in range(2)]
            )

        def store(e, value):
            grads_ref[256 + 8 * e:256 + 8 * e + 8, lanes] = value

        @pl.when(active)
        def _():
            level = iota((8, 128), 1) + first
            level = jnp.where(level >= 512, level - 512, level)
            column(level, half_order, half_ref[:, lanes], load, store)

        @pl.when(jnp.logical_not(active))
        def _():
            grads_ref[256:384, lanes] = jnp.zeros((128, 128), jnp.float32)

    grads_ref[0:256, 384:512] = jnp.zeros((256, 128), jnp.float32)
    total = total_ref[...]
    score = jnp.sum(jnp.sum(total, axis=1, keepdims=True), axis=0, keepdims=True)
    high = score.astype(jnp.bfloat16).astype(jnp.float32)
    middle = (score - high).astype(jnp.bfloat16).astype(jnp.float32)
    low = score - high - middle
    spot = iota((128, 128), 1)
    pieces = jnp.where(spot == 96, high, jnp.where(spot == 97, middle, jnp.where(spot == 98, low, 0.0)))

    waves_grad = lax.dot_general(
        grads_ref[...].astype(jnp.bfloat16), flat_ref[:, 384:896], (((1,), (1,)), ((), ())),
        preferred_element_type=jnp.float32,
    )
    for j in range(16):
        merged = pieces
        for w in range(3):
            block = waves_grad[128 * w:128 * w + 128, 128 * (j // 4):128 * (j // 4) + 128]
            turn = (w - j) % 4
            if turn:
                block = pltpu.roll(block, 32 * turn, 1)
            merged = jnp.where(spot // 32 == w, block, merged)
        back_ref[128 * j:128 * j + 128, :] = merged.astype(jnp.bfloat16)


def score_call(orders, got, full_rows, half_rows, limit):
    vmem = pl.BlockSpec(memory_space=pltpu.VMEM)
    return pl.pallas_call(
        score_kernel,
        out_shape=jax.ShapeDtypeStruct((2048, 128), jnp.bfloat16),
        in_specs=[pl.BlockSpec(memory_space=pltpu.SMEM), vmem, vmem, vmem, vmem],
        out_specs=vmem,
        scratch_shapes=[
            pltpu.VMEM((512, 896), jnp.bfloat16),
            pltpu.VMEM((384, 512), jnp.bfloat16),
            pltpu.VMEM((4, 384, 128), jnp.float32),
            pltpu.VMEM((384, 512), jnp.float32),
            pltpu.VMEM((8, 128), jnp.float32),
        ],
        compiler_params=pltpu.CompilerParams(vmem_limit_bytes=20 * 1024 * 1024),
    )(orders, got, full_rows, half_rows, limit)


def home_kernel(valid_ref, codes_ref, got_ref, waves_ref, score_ref, out_ref, mix_ref, turned_ref):
    mix_ref[...] = got_ref[...].astype(jnp.float32)
    for f in range(8):
        rows = mix_ref[pl.ds(f, 256, stride=8), :]
        if f == 0:
            spot = iota((256, 128), 1)
            pieces = jnp.where((spot >= 96) & (spot < 99), rows, 0.0)
            score_ref[0] = jnp.sum(pieces) / valid_ref[0]
        turned = jnp.transpose(rows, (1, 0)).astype(jnp.bfloat16)
        for w in range(3):
            turned_ref[w, 32 * f:32 * f + 32, :] = turned[32 * w:32 * w + 32]
    full, even, odd, _ = picks(codes_ref[0:1, :], codes_ref[1:2, :])
    first = dot(turned_ref[0], full) + dot(turned_ref[2], even)
    second = dot(turned_ref[1], full) + dot(turned_ref[2], odd)
    natural = jnp.concatenate([first, second], axis=1).astype(jnp.bfloat16)
    out_ref[...] = dot(natural, waves_ref[...]).astype(jnp.bfloat16)


def home_call(valid, codes, got, waves):
    vmem = pl.BlockSpec(memory_space=pltpu.VMEM)
    smem = pl.BlockSpec(memory_space=pltpu.SMEM)
    return pl.pallas_call(
        home_kernel,
        out_shape=(
            jax.ShapeDtypeStruct((1,), jnp.float32),
            jax.ShapeDtypeStruct((256, waves.shape[1]), jnp.bfloat16),
        ),
        in_specs=[smem, vmem, vmem, vmem],
        out_specs=(smem, vmem),
        scratch_shapes=[pltpu.VMEM((2048, 128), jnp.float32), pltpu.VMEM((3, 256, 256), jnp.bfloat16)],
        compiler_params=pltpu.CompilerParams(vmem_limit_bytes=20 * 1024 * 1024),
    )(valid, codes, got, waves)


def exchange(rows):
    return lax.all_to_all(rows, both_axes, split_axis=0, concat_axis=0, tiled=True)


def shift_of(order):
    return jnp.where(order >= 368, 0, (368 - order + 31) // 32 * 32)


def ranked(orders):
    rank = jnp.sum((orders[..., None] > orders[..., None, :]).astype(jnp.int32), axis=-1)
    return rank


def exact(equation, left, right):
    return jnp.einsum(equation, left, right, preferred_element_type=jnp.float32).astype(jnp.bfloat16)


def unpacked(grid, legendre, target, owner, cutoff, waves, modes_valid):
    fields, rows = grid.shape[1:3]
    modes, levels = legendre.shape[1:]
    e = lax.axis_index("ens")
    j = lax.axis_index("lat")
    natural = jnp.arange(modes, dtype=jnp.int32)
    place = jnp.arange(256, dtype=jnp.int32)
    full_slots = place // 16 * 24 + place % 16
    half_slots = place // 16 * 24 + 16 + place % 16 // 2
    pick_full = (owner[full_slots][:, None] == natural).astype(jnp.bfloat16)
    pick_half = (owner[half_slots][:, None] == natural).astype(jnp.bfloat16)
    zeros = jnp.zeros_like(pick_full)
    odd = (place % 2 == 1)[:, None]
    pick = jnp.stack([
        jnp.stack([pick_full, zeros], axis=1),
        jnp.stack([zeros, pick_full], axis=1),
        jnp.stack([jnp.where(odd, zeros, pick_half), jnp.where(odd, pick_half, zeros)], axis=1),
    ], axis=1)
    table = waves.reshape(2, modes, -1)
    fourier = exact("cmn,fan->cmfa", table, grid[0])
    fourier = exchange(exact("dwcm,cmfa->dwfa", pick, fourier).reshape(256, 6, 128))
    fourier = fourier.reshape(16, 16, 3, fields, rows)
    bands = lax.dynamic_slice_in_dim(legendre, 2 * e, 2, axis=0)
    pick_orders = jnp.stack([pick_full, pick_half], axis=1)
    weights = exchange(exact("dom,rml->drol", pick_orders, bands).reshape(256, 4, levels))
    weights = weights.reshape(16, rows, 2, levels)
    weights = jnp.stack([weights[:, :, 0], weights[:, :, 0], weights[:, :, 1]], axis=2)
    coeffs = jnp.einsum("jewfa,jawl->ewfl", fourier, weights, preferred_element_type=jnp.float32)

    own = lax.dynamic_slice_in_dim(owner, 24 * j, 24)
    full_rows = lax.dynamic_index_in_dim(target, e, 0, keepdims=False)
    half_rows = lax.dynamic_slice(target, (16 + e // 2, 0, e % 2, 0), (1, fields, 1, levels))[0, :, 0]
    goal = jnp.stack([full_rows[:, 0], full_rows[:, 1], half_rows])
    order = jnp.stack([own[e], own[e], own[16 + e // 2]])[:, None, None]
    level = jnp.arange(levels, dtype=jnp.int32)
    inside = ((level >= order) & (level <= cutoff[None, :, None])).astype(jnp.float32)
    offset = delta_abs * delta_abs
    spread = coeffs[:, None] - coeffs[None]
    height = jnp.sqrt(spread * spread + offset)
    pair_value = jnp.sum(height - delta_abs, axis=1)
    pair_slope = jnp.sum(spread / height, axis=1)
    spread = coeffs - goal
    height = jnp.sqrt(spread * spread + offset)
    score = jnp.sum(inside * ((height - delta_abs) / 16.0 - pair_value / 512.0))
    grad = (inside * (spread / height - pair_slope / 16.0)).astype(jnp.bfloat16)
    score = exchange(jnp.full((256, 1, 128), score, jnp.float32))
    mean_score = (jnp.sum(score[:, 0, 0]) / modes_valid[0]).reshape(1)

    back = exchange(exact("ewfl,jawl->jewfa", grad, weights).reshape(256, 6, 128))
    back = exact("dwcm,dwfa->facm", pick, back.reshape(256, 3, fields, rows))
    return mean_score, exact("facm,cmn->fan", back, table)[None]


def body(grid, legendre, target, owner, cutoff):
    fields, rows, lon_count = grid.shape[1:]
    modes = legendre.shape[1]
    e = lax.axis_index("ens")
    j = lax.axis_index("lat")
    table = wave_table(modes, lon_count).reshape(2 * modes, lon_count)
    waves = jnp.asarray(table)
    turned = jnp.asarray(np.ascontiguousarray(table.T))
    sent, codes = send_call(
        e.reshape(1), owner, grid.reshape(fields * rows, lon_count), turned, legendre
    )
    got = exchange(sent)

    by_lat = owner.reshape(16, 24)
    rank = ranked(by_lat)
    spots = jnp.arange(24, dtype=jnp.int32)
    by_rank = jnp.sum(jnp.where(rank[:, :, None] == spots, by_lat[:, :, None], 0), axis=1)
    long_orders = by_rank[:, 0:16:2]
    short_orders = by_rank[:, 23:15:-1]
    fits = jnp.all(360 + shift_of(short_orders) <= 511 + long_orders)

    own = lax.dynamic_slice_in_dim(owner, 24 * j, 24)
    own_rank = ranked(own)
    is_full = own_rank == e
    is_half = own_rank == 23 - e // 2
    full_order = jnp.sum(jnp.where(is_full, own, 0))
    half_order = jnp.sum(jnp.where(is_half, own, 0))
    shift = shift_of(half_order)
    orders = jnp.stack([full_order, half_order, shift, jnp.max(cutoff)])
    full_slot = jnp.sum(jnp.where(is_full, spots, 0))
    half_slot = jnp.sum(jnp.where(is_half, spots, 0))
    full_rows = lax.dynamic_index_in_dim(target, full_slot, 0, keepdims=False)
    full_rows = jnp.concatenate([full_rows[:, 0], full_rows[:, 1]])
    half_rows = lax.dynamic_slice(target, (half_slot, 0, e % 2, 0), (1, fields, 1, target.shape[3]))
    half_rows = jnp.pad(half_rows[0, :, 0], ((0, 0), (0, 512 - target.shape[3])))
    half_rows = lax.dynamic_slice_in_dim(jnp.concatenate([half_rows, half_rows], axis=1), 512 - shift, 512, axis=1)
    limit = jnp.broadcast_to(cutoff[:, None], (fields, 128))
    cut_level = cutoff.astype(jnp.float32)
    modes_valid = jnp.sum((cut_level + 1.0) * (cut_level + 2.0)).reshape(1)

    flag = fits.astype(jnp.int32)
    got, flag, modes_valid = lax.optimization_barrier((got, flag, modes_valid))
    back = score_call(orders, got, full_rows, half_rows, limit)
    home = exchange(back.reshape(256, 8, 128)).reshape(2048, 128)
    mean_score, grid_grad = home_call(modes_valid, codes, home, waves)
    grid_grad = grid_grad.reshape(1, fields, rows, lon_count)
    _, mean_score, grid_grad = lax.while_loop(
        lambda state: state[0] == 0,
        lambda state: (jnp.int32(1), *unpacked(grid, legendre, target, owner, cutoff, waves, modes_valid)),
        (flag, mean_score, grid_grad),
    )
    return mean_score, grid_grad


def solution(mesh):
    in_specs = (
        P("ens", None, "lat", None),
        P("lat", None, None),
        P("lat", None, None, None),
        P(),
        P(),
    )
    out_specs = (P(), P("ens", None, "lat", None))
    return jax.shard_map(body, mesh=mesh, in_specs=in_specs, out_specs=out_specs, check_vma=False)
```

```python
import math

import jax
import jax.numpy as jnp
import numpy as np
from jax import lax
from jax.experimental import pallas as pl
from jax.experimental.pallas import tpu as pltpu
from jax.sharding import PartitionSpec as P

delta_abs = 0.1
both_axes = ("lat", "ens")


def wave_table(mode_count, lon_count):
    points = np.arange(lon_count, dtype=np.int64)
    modes = np.arange(mode_count, dtype=np.int64)
    phase = modes[:, None] * points[None, :] % lon_count
    angle = phase.astype(np.float32) * np.float32(2.0 * math.pi / lon_count)
    both = np.stack([np.cos(angle), -np.sin(angle)]) / np.float32(math.sqrt(lon_count))
    return both.astype(np.float32).astype(jnp.bfloat16)


def dot(left, right):
    return jnp.dot(left, right, preferred_element_type=jnp.float32)


def flag(condition):
    return jnp.where(condition, 1.0, 0.0).astype(jnp.bfloat16)


def iota(shape, axis):
    return lax.broadcasted_iota(jnp.int32, shape, axis)


def send_kernel(
    place_ref, owner_hbm, grid_hbm, waves_hbm, legendre_hbm, out_ref, codes_ref,
    owner_ref, grid_ref, waves_ref, bands_ref, table_ref, four_ref, mix_ref, sems,
):
    grid_copy = pltpu.make_async_copy(grid_hbm, grid_ref, sems.at[0])
    band_copy = pltpu.make_async_copy(
        legendre_hbm.at[pl.ds(2 * place_ref[0], 2)], bands_ref, sems.at[1]
    )
    wave_copies = [
        pltpu.make_async_copy(
            waves_hbm.at[:, pl.ds(384 * c, 384)], waves_ref.at[:, pl.ds(384 * c, 384)], sems.at[2 + c]
        )
        for c in range(2)
    ]
    owner_copy = pltpu.make_async_copy(owner_hbm, owner_ref, sems.at[4])
    owner_copy.start()
    band_copy.start()
    grid_copy.start()
    for copy in wave_copies:
        copy.start()

    owner_copy.wait()
    line = jnp.broadcast_to(owner_ref[...].reshape(1, 384).astype(jnp.float32), (128, 384))
    column = jnp.transpose(line, (1, 0))
    lane = iota((384, 128), 1).astype(jnp.float32)
    held = jnp.concatenate([flag(column == lane + 128.0 * t) for t in range(3)], axis=1)
    group = flag(iota((16, 384), 1) // 24 == iota((16, 384), 0))
    lat_of = dot(group, held)
    before = flag(iota((384, 384), 0) < iota((384, 384), 1))
    count = dot(lat_of.astype(jnp.bfloat16), before)
    rank = jnp.sum(lat_of * count, axis=0, keepdims=True)
    lat = jnp.sum(lat_of * iota((16, 384), 0).astype(jnp.float32), axis=0, keepdims=True)
    full_code = jnp.where(rank < 16.0, lat * 16.0 + rank, -1.0)
    half_code = jnp.where(rank >= 16.0, lat * 8.0 + (23.0 - rank), -1.0)
    codes_ref[0:1, :] = full_code
    codes_ref[1:2, :] = half_code
    codes_ref[2:8, :] = jnp.zeros((6, 384), jnp.float32)
    full, even, odd, half = picks(full_code, half_code)

    both = jnp.concatenate([full, half], axis=1)
    band_copy.wait()
    for r in range(2):
        rows = bands_ref[r]
        table_ref[0:384, 0:384] = rows
        table_ref[0:384, 384:512] = jnp.zeros((384, 128), jnp.bfloat16)
        wide = jnp.concatenate([rows.astype(jnp.float32), jnp.zeros((384, 128), jnp.float32)], axis=1)
        table_ref[384 + 368:768, :] = wide[368:384].astype(jnp.bfloat16)
        for step in range(1, 24):
            low = 368 - 16 * step
            moved = pltpu.roll(wide[low:low + 16], 16 * step, 1)
            table_ref[384 + low:384 + low + 16, :] = moved.astype(jnp.bfloat16)
        packed = dot(both, table_ref[...])
        for t in range(4):
            mix_ref[3 + t, pl.ds(r, 256, stride=2), :] = packed[:, 128 * t:128 * t + 128]

    for t in range(3, 7):
        out_ref[:, :, 128 * t:128 * t + 128] = mix_ref[t].astype(jnp.bfloat16).reshape(256, 2, 128)

    dims = (((1,), (1,)), ((), ()))
    grid_copy.wait()
    for c in range(2):
        wave_copies[c].wait()
        columns = slice(384 * c, 384 * c + 384)
        four_ref[:, columns] = dot(grid_ref[...], waves_ref[:, columns]).astype(jnp.bfloat16)
        part = lax.dot_general(full, four_ref[:, columns], dims, preferred_element_type=jnp.float32)
        for h in range(2):
            mix_ref[h, pl.ds(c, 256, stride=2), :] = part[:, 128 * h:128 * h + 128]
    part = lax.dot_general(
        jnp.concatenate([even, odd], axis=1), four_ref[...], dims, preferred_element_type=jnp.float32
    )
    for h in range(2):
        mix_ref[2, pl.ds(h, 256, stride=2), :] = part[:, 128 * h:128 * h + 128]
    for t in range(3):
        out_ref[:, :, 128 * t:128 * t + 128] = mix_ref[t].astype(jnp.bfloat16).reshape(256, 2, 128)


def picks(full_code, half_code):
    row = iota((256, 384), 0)
    full = flag(row.astype(jnp.float32) == full_code)
    match = (row // 2).astype(jnp.float32) == half_code
    even = flag(match & (row % 2 == 0))
    odd = flag(match & (row % 2 == 1))
    return full, even, odd, flag(match)


def send_call(place, owner, grid, waves, legendre):
    vmem = pl.BlockSpec(memory_space=pltpu.VMEM)
    anywhere = pl.BlockSpec(memory_space=pltpu.HBM)
    return pl.pallas_call(
        send_kernel,
        out_shape=(
            jax.ShapeDtypeStruct((256, 2, 896), jnp.bfloat16),
            jax.ShapeDtypeStruct((8, 384), jnp.float32),
        ),
        in_specs=[pl.BlockSpec(memory_space=pltpu.SMEM), anywhere, anywhere, anywhere, anywhere],
        out_specs=(vmem, vmem),
        scratch_shapes=[
            pltpu.VMEM((384,), jnp.int32),
            pltpu.VMEM((256, 1440), jnp.bfloat16),
            pltpu.VMEM((1440, 768), jnp.bfloat16),
            pltpu.VMEM((2, 384, 384), jnp.bfloat16),
            pltpu.VMEM((768, 512), jnp.bfloat16),
            pltpu.VMEM((256, 768), jnp.bfloat16),
            pltpu.VMEM((7, 512, 128), jnp.float32),
            pltpu.SemaphoreType.DMA((5,)),
        ],
        compiler_params=pltpu.CompilerParams(vmem_limit_bytes=58 * 1024 * 1024),
    )(place, owner, grid, waves, legendre)


def score_kernel(
    orders_ref, got_ref, full_ref, half_ref, cutoff_ref, back_ref,
    flat_ref, rows_ref, coeffs_ref, grads_ref, total_ref,
):
    flat_ref[...] = got_ref[...].reshape(512, 896)
    lane_group = iota((32, 128), 1) // 32
    for q in range(3):
        for group in range(4):
            blocks = [
                flat_ref[128 * group + 32 * i:128 * group + 32 * i + 32, 128 * q:128 * q + 128].astype(jnp.float32)
                for i in range(4)
            ]
            for k in range(4):
                merged = jnp.zeros((32, 128), jnp.float32)
                for i in range(4):
                    turn = (i - k) % 4
                    block = pltpu.roll(blocks[i], 32 * turn, 1) if turn else blocks[i]
                    merged = jnp.where(lane_group == i, block, merged)
                row = (q * 4 + k) * 32
                rows_ref[row:row + 32, 128 * group:128 * group + 128] = merged.astype(jnp.bfloat16)
    coeffs = dot(rows_ref[...], flat_ref[:, 384:896])
    for t in range(4):
        coeffs_ref[t] = coeffs[:, 128 * t:128 * t + 128]
    offset = delta_abs * delta_abs
    limit = cutoff_ref[...]

    def column(level, order, goal, load, store):
        inside = (level >= order) & (level <= limit)
        member = [load(e) for e in range(16)]
        slope = [jnp.zeros((8, 128), jnp.float32) for _ in range(16)]
        rest = jnp.zeros((8, 128), jnp.float32)
        for i in range(16):
            for k in range(i + 1, 16):
                spread = member[i] - member[k]
                inverse = lax.rsqrt(spread * spread + offset)
                step_slope = spread * inverse
                slope[i] = slope[i] + step_slope
                slope[k] = slope[k] - step_slope
                rest = rest + (inverse - 1.0 / delta_abs)
        pair_value = offset * rest
        for i in range(1, 16):
            pair_value = pair_value + (member[i] - member[0]) * slope[i]
        own_value = jnp.zeros((8, 128), jnp.float32)
        for i in range(16):
            spread = member[i] - goal
            square = spread * spread + offset
            inverse = lax.rsqrt(square)
            own_value = own_value + (square * inverse - delta_abs)
            store(i, jnp.where(inside, spread * inverse - slope[i] / 16.0, 0.0))
        total_ref[...] += jnp.where(inside, own_value / 16.0 - pair_value / 256.0, 0.0)

    total_ref[...] = jnp.zeros((8, 128), jnp.float32)
    full_order, half_order, shift, highest = [orders_ref[i] for i in range(4)]

    @pl.loop(0, 6)
    def _(step):
        part = step // 3
        third = step % 3
        lanes = pl.ds(pl.multiple_of(third * 128, 128), 128)
        first = third * 128
        active = (first + 127 >= full_order) & (first <= highest)

        def load(e):
            return coeffs_ref[third, pl.ds(2 * e + part, 8, stride=32), :]

        def store(e, value):
            grads_ref[pl.ds(pl.multiple_of(part * 128 + 8 * e, 8), 8), lanes] = value

        @pl.when(active)
        def _():
            goal = full_ref[pl.ds(pl.multiple_of(part * 8, 8), 8), lanes]
            column(iota((8, 128), 1) + first, full_order, goal, load, store)

        @pl.when(jnp.logical_not(active))
        def _():
            grads_ref[pl.ds(pl.multiple_of(part * 128, 128), 128), lanes] = jnp.zeros((128, 128), jnp.float32)

    @pl.loop(0, 4)
    def _(tile):
        lanes = pl.ds(pl.multiple_of(tile * 128, 128), 128)
        first = tile * 128 - shift
        first = jnp.where(first < 0, first + 512, first)
        active = ((first + 127 >= half_order) & (first <= highest)) | (first - 385 >= half_order)

        def load(e):
            return jnp.concatenate(
                [coeffs_ref[tile, pl.ds(256 + 2 * e + h, 4, stride=32), :] for h in range(2)]
            )

        def store(e, value):
            grads_ref[256 + 8 * e:256 + 8 * e + 8, lanes] = value

        @pl.when(active)
        def _():
            level = iota((8, 128), 1) + first
            level = jnp.where(level >= 512, level - 512, level)
            column(level, half_order, half_ref[:, lanes], load, store)

        @pl.when(jnp.logical_not(active))
        def _():
            grads_ref[256:384, lanes] = jnp.zeros((128, 128), jnp.float32)

    grads_ref[0:256, 384:512] = jnp.zeros((256, 128), jnp.float32)
    total = total_ref[...]
    score = jnp.sum(jnp.sum(total, axis=1, keepdims=True), axis=0, keepdims=True)
    high = score.astype(jnp.bfloat16).astype(jnp.float32)
    middle = (score - high).astype(jnp.bfloat16).astype(jnp.float32)
    low = score - high - middle
    spot = iota((128, 128), 1)
    pieces = jnp.where(spot == 96, high, jnp.where(spot == 97, middle, jnp.where(spot == 98, low, 0.0)))

    waves_grad = lax.dot_general(
        grads_ref[...].astype(jnp.bfloat16), flat_ref[:, 384:896], (((1,), (1,)), ((), ())),
        preferred_element_type=jnp.float32,
    )
    for j in range(16):
        merged = pieces
        for w in range(3):
            block = waves_grad[128 * w:128 * w + 128, 128 * (j // 4):128 * (j // 4) + 128]
            turn = (w - j) % 4
            if turn:
                block = pltpu.roll(block, 32 * turn, 1)
            merged = jnp.where(spot // 32 == w, block, merged)
        back_ref[128 * j:128 * j + 128, :] = merged.astype(jnp.bfloat16)


def score_call(orders, got, full_rows, half_rows, limit):
    vmem = pl.BlockSpec(memory_space=pltpu.VMEM)
    return pl.pallas_call(
        score_kernel,
        out_shape=jax.ShapeDtypeStruct((2048, 128), jnp.bfloat16),
        in_specs=[pl.BlockSpec(memory_space=pltpu.SMEM), vmem, vmem, vmem, vmem],
        out_specs=vmem,
        scratch_shapes=[
            pltpu.VMEM((512, 896), jnp.bfloat16),
            pltpu.VMEM((384, 512), jnp.bfloat16),
            pltpu.VMEM((4, 384, 128), jnp.float32),
            pltpu.VMEM((384, 512), jnp.float32),
            pltpu.VMEM((8, 128), jnp.float32),
        ],
        compiler_params=pltpu.CompilerParams(vmem_limit_bytes=20 * 1024 * 1024),
    )(orders, got, full_rows, half_rows, limit)


def home_kernel(valid_ref, codes_ref, got_ref, waves_ref, score_ref, out_ref, mix_ref, turned_ref):
    mix_ref[...] = got_ref[...].astype(jnp.float32)
    for f in range(8):
        rows = mix_ref[pl.ds(f, 256, stride=8), :]
        if f == 0:
            spot = iota((256, 128), 1)
            pieces = jnp.where((spot >= 96) & (spot < 99), rows, 0.0)
            score_ref[0] = jnp.sum(pieces) / valid_ref[0]
        turned = jnp.transpose(rows, (1, 0)).astype(jnp.bfloat16)
        for w in range(3):
            turned_ref[w, 32 * f:32 * f + 32, :] = turned[32 * w:32 * w + 32]
    full, even, odd, _ = picks(codes_ref[0:1, :], codes_ref[1:2, :])
    first = dot(turned_ref[0], full) + dot(turned_ref[2], even)
    second = dot(turned_ref[1], full) + dot(turned_ref[2], odd)
    natural = jnp.concatenate([first, second], axis=1).astype(jnp.bfloat16)
    out_ref[...] = dot(natural, waves_ref[...]).astype(jnp.bfloat16)


def home_call(valid, codes, got, waves):
    vmem = pl.BlockSpec(memory_space=pltpu.VMEM)
    smem = pl.BlockSpec(memory_space=pltpu.SMEM)
    return pl.pallas_call(
        home_kernel,
        out_shape=(
            jax.ShapeDtypeStruct((1,), jnp.float32),
            jax.ShapeDtypeStruct((256, waves.shape[1]), jnp.bfloat16),
        ),
        in_specs=[smem, vmem, vmem, vmem],
        out_specs=(smem, vmem),
        scratch_shapes=[pltpu.VMEM((2048, 128), jnp.float32), pltpu.VMEM((3, 256, 256), jnp.bfloat16)],
        compiler_params=pltpu.CompilerParams(vmem_limit_bytes=20 * 1024 * 1024),
    )(valid, codes, got, waves)


def exchange(rows):
    return lax.all_to_all(rows, both_axes, split_axis=0, concat_axis=0, tiled=True)


def shift_of(order):
    return jnp.where(order >= 368, 0, (368 - order + 15) // 16 * 16)


def ranked(orders):
    rank = jnp.sum((orders[..., None] > orders[..., None, :]).astype(jnp.int32), axis=-1)
    return rank


def exact(equation, left, right):
    return jnp.einsum(equation, left, right, preferred_element_type=jnp.float32).astype(jnp.bfloat16)


def unpacked(grid, legendre, target, owner, cutoff, waves, modes_valid):
    fields, rows = grid.shape[1:3]
    modes, levels = legendre.shape[1:]
    e = lax.axis_index("ens")
    j = lax.axis_index("lat")
    natural = jnp.arange(modes, dtype=jnp.int32)
    place = jnp.arange(256, dtype=jnp.int32)
    full_slots = place // 16 * 24 + place % 16
    half_slots = place // 16 * 24 + 16 + place % 16 // 2
    pick_full = (owner[full_slots][:, None] == natural).astype(jnp.bfloat16)
    pick_half = (owner[half_slots][:, None] == natural).astype(jnp.bfloat16)
    zeros = jnp.zeros_like(pick_full)
    odd = (place % 2 == 1)[:, None]
    pick = jnp.stack([
        jnp.stack([pick_full, zeros], axis=1),
        jnp.stack([zeros, pick_full], axis=1),
        jnp.stack([jnp.where(odd, zeros, pick_half), jnp.where(odd, pick_half, zeros)], axis=1),
    ], axis=1)
    table = waves.reshape(2, modes, -1)
    fourier = exact("cmn,fan->cmfa", table, grid[0])
    fourier = exchange(exact("dwcm,cmfa->dwfa", pick, fourier).reshape(256, 6, 128))
    fourier = fourier.reshape(16, 16, 3, fields, rows)
    bands = lax.dynamic_slice_in_dim(legendre, 2 * e, 2, axis=0)
    pick_orders = jnp.stack([pick_full, pick_half], axis=1)
    weights = exchange(exact("dom,rml->drol", pick_orders, bands).reshape(256, 4, levels))
    weights = weights.reshape(16, rows, 2, levels)
    weights = jnp.stack([weights[:, :, 0], weights[:, :, 0], weights[:, :, 1]], axis=2)
    coeffs = jnp.einsum("jewfa,jawl->ewfl", fourier, weights, preferred_element_type=jnp.float32)

    own = lax.dynamic_slice_in_dim(owner, 24 * j, 24)
    full_rows = lax.dynamic_index_in_dim(target, e, 0, keepdims=False)
    half_rows = lax.dynamic_slice(target, (16 + e // 2, 0, e % 2, 0), (1, fields, 1, levels))[0, :, 0]
    goal = jnp.stack([full_rows[:, 0], full_rows[:, 1], half_rows])
    order = jnp.stack([own[e], own[e], own[16 + e // 2]])[:, None, None]
    level = jnp.arange(levels, dtype=jnp.int32)
    inside = ((level >= order) & (level <= cutoff[None, :, None])).astype(jnp.float32)
    offset = delta_abs * delta_abs
    spread = coeffs[:, None] - coeffs[None]
    height = jnp.sqrt(spread * spread + offset)
    pair_value = jnp.sum(height - delta_abs, axis=1)
    pair_slope = jnp.sum(spread / height, axis=1)
    spread = coeffs - goal
    height = jnp.sqrt(spread * spread + offset)
    score = jnp.sum(inside * ((height - delta_abs) / 16.0 - pair_value / 512.0))
    grad = (inside * (spread / height - pair_slope / 16.0)).astype(jnp.bfloat16)
    score = exchange(jnp.full((256, 1, 128), score, jnp.float32))
    mean_score = (jnp.sum(score[:, 0, 0]) / modes_valid[0]).reshape(1)

    back = exchange(exact("ewfl,jawl->jewfa", grad, weights).reshape(256, 6, 128))
    back = exact("dwcm,dwfa->facm", pick, back.reshape(256, 3, fields, rows))
    return mean_score, exact("facm,cmn->fan", back, table)[None]


def body(grid, legendre, target, owner, cutoff):
    fields, rows, lon_count = grid.shape[1:]
    modes = legendre.shape[1]
    e = lax.axis_index("ens")
    j = lax.axis_index("lat")
    table = wave_table(modes, lon_count).reshape(2 * modes, lon_count)
    waves = jnp.asarray(table)
    turned = jnp.asarray(np.ascontiguousarray(table.T))
    sent, codes = send_call(
        e.reshape(1), owner, grid.reshape(fields * rows, lon_count), turned, legendre
    )
    got = exchange(sent)

    by_lat = owner.reshape(16, 24)
    rank = ranked(by_lat)
    spots = jnp.arange(24, dtype=jnp.int32)
    by_rank = jnp.sum(jnp.where(rank[:, :, None] == spots, by_lat[:, :, None], 0), axis=1)
    long_orders = by_rank[:, 0:16:2]
    short_orders = by_rank[:, 23:15:-1]
    fits = jnp.all(360 + shift_of(short_orders) <= 511 + long_orders)

    own = lax.dynamic_slice_in_dim(owner, 24 * j, 24)
    own_rank = ranked(own)
    is_full = own_rank == e
    is_half = own_rank == 23 - e // 2
    full_order = jnp.sum(jnp.where(is_full, own, 0))
    half_order = jnp.sum(jnp.where(is_half, own, 0))
    shift = shift_of(half_order)
    orders = jnp.stack([full_order, half_order, shift, jnp.max(cutoff)])
    full_slot = jnp.sum(jnp.where(is_full, spots, 0))
    half_slot = jnp.sum(jnp.where(is_half, spots, 0))
    full_rows = lax.dynamic_index_in_dim(target, full_slot, 0, keepdims=False)
    full_rows = jnp.concatenate([full_rows[:, 0], full_rows[:, 1]])
    half_rows = lax.dynamic_slice(target, (half_slot, 0, e % 2, 0), (1, fields, 1, target.shape[3]))
    half_rows = jnp.pad(half_rows[0, :, 0], ((0, 0), (0, 512 - target.shape[3])))
    half_rows = lax.dynamic_slice_in_dim(jnp.concatenate([half_rows, half_rows], axis=1), 512 - shift, 512, axis=1)
    limit = jnp.broadcast_to(cutoff[:, None], (fields, 128))
    cut_level = cutoff.astype(jnp.float32)
    modes_valid = jnp.sum((cut_level + 1.0) * (cut_level + 2.0)).reshape(1)

    flag = fits.astype(jnp.int32)
    got, flag, modes_valid = lax.optimization_barrier((got, flag, modes_valid))
    back = score_call(orders, got, full_rows, half_rows, limit)
    home = exchange(back.reshape(256, 8, 128)).reshape(2048, 128)
    mean_score, grid_grad = home_call(modes_valid, codes, home, waves)
    grid_grad = grid_grad.reshape(1, fields, rows, lon_count)
    _, mean_score, grid_grad = lax.while_loop(
        lambda state: state[0] == 0,
        lambda state: (jnp.int32(1), *unpacked(grid, legendre, target, owner, cutoff, waves, modes_valid)),
        (flag, mean_score, grid_grad),
    )
    return mean_score, grid_grad


def solution(mesh):
    in_specs = (
        P("ens", None, "lat", None),
        P("lat", None, None),
        P("lat", None, None, None),
        P(),
        P(),
    )
    out_specs = (P(), P("ens", None, "lat", None))
    return jax.shard_map(body, mesh=mesh, in_specs=in_specs, out_specs=out_specs, check_vma=False)
```

```python
import math

import jax
import jax.numpy as jnp
import numpy as np
from jax import lax
from jax.experimental import pallas as pl
from jax.experimental.pallas import tpu as pltpu
from jax.sharding import PartitionSpec as P

delta_abs = 0.1
both_axes = ("lat", "ens")


def wave_table(mode_count, lon_count):
    points = np.arange(lon_count, dtype=np.int64)
    modes = np.arange(mode_count, dtype=np.int64)
    phase = modes[:, None] * points[None, :] % lon_count
    angle = phase.astype(np.float32) * np.float32(2.0 * math.pi / lon_count)
    both = np.stack([np.cos(angle), -np.sin(angle)]) / np.float32(math.sqrt(lon_count))
    return both.astype(np.float32).astype(jnp.bfloat16)


def dot(left, right):
    return jnp.dot(left, right, preferred_element_type=jnp.float32)


def flag(condition):
    return jnp.where(condition, 1.0, 0.0).astype(jnp.bfloat16)


def iota(shape, axis):
    return lax.broadcasted_iota(jnp.int32, shape, axis)


def send_kernel(
    place_ref, owner_hbm, grid_hbm, waves_hbm, legendre_hbm, out_ref, codes_ref,
    owner_ref, grid_ref, waves_ref, bands_ref, table_ref, four_ref, mix_ref, sems,
):
    grid_copy = pltpu.make_async_copy(grid_hbm, grid_ref, sems.at[0])
    band_copy = pltpu.make_async_copy(
        legendre_hbm.at[pl.ds(2 * place_ref[0], 2)], bands_ref, sems.at[1]
    )
    wave_copies = [
        pltpu.make_async_copy(
            waves_hbm.at[:, pl.ds(384 * c, 384)], waves_ref.at[:, pl.ds(384 * c, 384)], sems.at[2 + c]
        )
        for c in range(2)
    ]
    owner_copy = pltpu.make_async_copy(owner_hbm, owner_ref, sems.at[4])
    owner_copy.start()
    band_copy.start()
    grid_copy.start()
    for copy in wave_copies:
        copy.start()

    group = flag(iota((16, 384), 1) // 24 == iota((16, 384), 0))
    before = flag(iota((384, 384), 0) < iota((384, 384), 1))
    table_ref[0:384, 384:512] = jnp.zeros((384, 128), jnp.bfloat16)
    codes_ref[2:8, :] = jnp.zeros((6, 384), jnp.float32)
    owner_copy.wait()
    line = jnp.broadcast_to(owner_ref[...].reshape(1, 384).astype(jnp.float32), (128, 384))
    column = jnp.transpose(line, (1, 0))
    lane = iota((384, 128), 1).astype(jnp.float32)
    held = jnp.concatenate([flag(column == lane + 128.0 * t) for t in range(3)], axis=1)
    lat_of = dot(group, held)
    count = dot(lat_of.astype(jnp.bfloat16), before)
    rank = jnp.sum(lat_of * count, axis=0, keepdims=True)
    lat = jnp.sum(lat_of * iota((16, 384), 0).astype(jnp.float32), axis=0, keepdims=True)
    full_code = jnp.where(rank < 16.0, lat * 16.0 + rank, -1.0)
    half_code = jnp.where(rank >= 16.0, lat * 8.0 + (23.0 - rank), -1.0)
    codes_ref[0:1, :] = full_code
    codes_ref[1:2, :] = half_code
    full, even, odd, half = picks(full_code, half_code)

    both = jnp.concatenate([full, half], axis=1)
    band_copy.wait()
    for r in range(2):
        rows = bands_ref[r]
        table_ref[0:384, 0:384] = rows
        wide = jnp.concatenate([rows.astype(jnp.float32), jnp.zeros((384, 128), jnp.float32)], axis=1)
        table_ref[384 + 368:768, :] = wide[368:384].astype(jnp.bfloat16)
        for step in range(1, 24):
            low = 368 - 16 * step
            moved = pltpu.roll(wide[low:low + 16], 16 * step, 1)
            table_ref[384 + low:384 + low + 16, :] = moved.astype(jnp.bfloat16)
        packed = dot(both, table_ref[...])
        for t in range(4):
            mix_ref[3 + t, pl.ds(r, 256, stride=2), :] = packed[:, 128 * t:128 * t + 128]

    for t in range(3, 7):
        out_ref[:, :, 128 * t:128 * t + 128] = mix_ref[t].astype(jnp.bfloat16).reshape(256, 2, 128)

    dims = (((1,), (1,)), ((), ()))
    grid_copy.wait()
    for c in range(2):
        wave_copies[c].wait()
        columns = slice(384 * c, 384 * c + 384)
        four_ref[:, columns] = dot(grid_ref[...], waves_ref[:, columns]).astype(jnp.bfloat16)
        part = lax.dot_general(full, four_ref[:, columns], dims, preferred_element_type=jnp.float32)
        for h in range(2):
            mix_ref[h, pl.ds(c, 256, stride=2), :] = part[:, 128 * h:128 * h + 128]
    part = lax.dot_general(
        jnp.concatenate([even, odd], axis=1), four_ref[...], dims, preferred_element_type=jnp.float32
    )
    for h in range(2):
        mix_ref[2, pl.ds(h, 256, stride=2), :] = part[:, 128 * h:128 * h + 128]
    for t in range(3):
        out_ref[:, :, 128 * t:128 * t + 128] = mix_ref[t].astype(jnp.bfloat16).reshape(256, 2, 128)


def picks(full_code, half_code):
    row = iota((256, 384), 0)
    full = flag(row.astype(jnp.float32) == full_code)
    match = (row // 2).astype(jnp.float32) == half_code
    even = flag(match & (row % 2 == 0))
    odd = flag(match & (row % 2 == 1))
    return full, even, odd, flag(match)


def send_call(place, owner, grid, waves, legendre):
    vmem = pl.BlockSpec(memory_space=pltpu.VMEM)
    anywhere = pl.BlockSpec(memory_space=pltpu.HBM)
    return pl.pallas_call(
        send_kernel,
        out_shape=(
            jax.ShapeDtypeStruct((256, 2, 896), jnp.bfloat16),
            jax.ShapeDtypeStruct((8, 384), jnp.float32),
        ),
        in_specs=[pl.BlockSpec(memory_space=pltpu.SMEM), anywhere, anywhere, anywhere, anywhere],
        out_specs=(vmem, vmem),
        scratch_shapes=[
            pltpu.VMEM((384,), jnp.int32),
            pltpu.VMEM((256, 1440), jnp.bfloat16),
            pltpu.VMEM((1440, 768), jnp.bfloat16),
            pltpu.VMEM((2, 384, 384), jnp.bfloat16),
            pltpu.VMEM((768, 512), jnp.bfloat16),
            pltpu.VMEM((256, 768), jnp.bfloat16),
            pltpu.VMEM((7, 512, 128), jnp.float32),
            pltpu.SemaphoreType.DMA((5,)),
        ],
        compiler_params=pltpu.CompilerParams(vmem_limit_bytes=58 * 1024 * 1024),
    )(place, owner, grid, waves, legendre)


def score_kernel(
    orders_ref, got_ref, full_ref, half_ref, cutoff_ref, back_ref,
    flat_ref, rows_ref, coeffs_ref, grads_ref, total_ref,
):
    flat_ref[...] = got_ref[...].reshape(512, 896)
    lane_group = iota((32, 128), 1) // 32
    for q in range(3):
        for group in range(4):
            blocks = [
                flat_ref[128 * group + 32 * i:128 * group + 32 * i + 32, 128 * q:128 * q + 128].astype(jnp.float32)
                for i in range(4)
            ]
            for k in range(4):
                merged = jnp.zeros((32, 128), jnp.float32)
                for i in range(4):
                    turn = (i - k) % 4
                    block = pltpu.roll(blocks[i], 32 * turn, 1) if turn else blocks[i]
                    merged = jnp.where(lane_group == i, block, merged)
                row = (q * 4 + k) * 32
                rows_ref[row:row + 32, 128 * group:128 * group + 128] = merged.astype(jnp.bfloat16)
    coeffs = dot(rows_ref[...], flat_ref[:, 384:896])
    for t in range(4):
        coeffs_ref[t] = coeffs[:, 128 * t:128 * t + 128]
    offset = delta_abs * delta_abs
    limit = cutoff_ref[...]

    def column(level, order, goal, load, store):
        inside = (level >= order) & (level <= limit)
        member = [load(e) for e in range(16)]
        slope = [jnp.zeros((8, 128), jnp.float32) for _ in range(16)]
        rest = jnp.zeros((8, 128), jnp.float32)
        for i in range(16):
            for k in range(i + 1, 16):
                spread = member[i] - member[k]
                inverse = lax.rsqrt(spread * spread + offset)
                step_slope = spread * inverse
                slope[i] = slope[i] + step_slope
                slope[k] = slope[k] - step_slope
                rest = rest + (inverse - 1.0 / delta_abs)
        pair_value = offset * rest
        for i in range(1, 16):
            pair_value = pair_value + (member[i] - member[0]) * slope[i]
        own_value = jnp.zeros((8, 128), jnp.float32)
        for i in range(16):
            spread = member[i] - goal
            square = spread * spread + offset
            inverse = lax.rsqrt(square)
            own_value = own_value + (square * inverse - delta_abs)
            store(i, jnp.where(inside, spread * inverse - slope[i] / 16.0, 0.0))
        total_ref[...] += jnp.where(inside, own_value / 16.0 - pair_value / 256.0, 0.0)

    total_ref[...] = jnp.zeros((8, 128), jnp.float32)
    full_order, half_order, shift, highest = [orders_ref[i] for i in range(4)]

    def full_step(step):
        part = step // 3
        third = step % 3
        lanes = pl.ds(third * 128, 128)
        first = third * 128
        active = (first + 127 >= full_order) & (first <= highest)

        def load(e):
            return coeffs_ref[third, pl.ds(2 * e + part, 8, stride=32), :]

        def store(e, value):
            grads_ref[pl.ds(part * 128 + 8 * e, 8), lanes] = value

        @pl.when(active)
        def _():
            goal = full_ref[pl.ds(part * 8, 8), lanes]
            column(iota((8, 128), 1) + first, full_order, goal, load, store)

        @pl.when(jnp.logical_not(active))
        def _():
            grads_ref[pl.ds(part * 128, 128), lanes] = jnp.zeros((128, 128), jnp.float32)

    for step in range(6):
        full_step(step)

    @pl.loop(0, 4)
    def _(tile):
        lanes = pl.ds(pl.multiple_of(tile * 128, 128), 128)
        first = tile * 128 - shift
        first = jnp.where(first < 0, first + 512, first)
        active = ((first + 127 >= half_order) & (first <= highest)) | (first - 385 >= half_order)

        def load(e):
            return jnp.concatenate(
                [coeffs_ref[tile, pl.ds(256 + 2 * e + h, 4, stride=32), :] for h in range(2)]
            )

        def store(e, value):
            grads_ref[256 + 8 * e:256 + 8 * e + 8, lanes] = value

        @pl.when(active)
        def _():
            level = iota((8, 128), 1) + first
            level = jnp.where(level >= 512, level - 512, level)
            column(level, half_order, half_ref[:, lanes], load, store)

        @pl.when(jnp.logical_not(active))
        def _():
            grads_ref[256:384, lanes] = jnp.zeros((128, 128), jnp.float32)

    grads_ref[0:256, 384:512] = jnp.zeros((256, 128), jnp.float32)
    total = total_ref[...]
    score = jnp.sum(jnp.sum(total, axis=1, keepdims=True), axis=0, keepdims=True)
    high = score.astype(jnp.bfloat16).astype(jnp.float32)
    middle = (score - high).astype(jnp.bfloat16).astype(jnp.float32)
    low = score - high - middle
    spot = iota((128, 128), 1)
    pieces = jnp.where(spot == 96, high, jnp.where(spot == 97, middle, jnp.where(spot == 98, low, 0.0)))

    waves_grad = lax.dot_general(
        grads_ref[...].astype(jnp.bfloat16), flat_ref[:, 384:896], (((1,), (1,)), ((), ())),
        preferred_element_type=jnp.float32,
    )
    for j in range(16):
        merged = pieces
        for w in range(3):
            block = waves_grad[128 * w:128 * w + 128, 128 * (j // 4):128 * (j // 4) + 128]
            turn = (w - j) % 4
            if turn:
                block = pltpu.roll(block, 32 * turn, 1)
            merged = jnp.where(spot // 32 == w, block, merged)
        back_ref[128 * j:128 * j + 128, :] = merged.astype(jnp.bfloat16)


def score_call(orders, got, full_rows, half_rows, limit):
    vmem = pl.BlockSpec(memory_space=pltpu.VMEM)
    return pl.pallas_call(
        score_kernel,
        out_shape=jax.ShapeDtypeStruct((2048, 128), jnp.bfloat16),
        in_specs=[pl.BlockSpec(memory_space=pltpu.SMEM), vmem, vmem, vmem, vmem],
        out_specs=vmem,
        scratch_shapes=[
            pltpu.VMEM((512, 896), jnp.bfloat16),
            pltpu.VMEM((384, 512), jnp.bfloat16),
            pltpu.VMEM((4, 384, 128), jnp.float32),
            pltpu.VMEM((384, 512), jnp.float32),
            pltpu.VMEM((8, 128), jnp.float32),
        ],
        compiler_params=pltpu.CompilerParams(vmem_limit_bytes=20 * 1024 * 1024),
    )(orders, got, full_rows, half_rows, limit)


def home_kernel(valid_ref, codes_ref, got_ref, waves_ref, score_ref, out_ref, mix_ref, turned_ref):
    mix_ref[...] = got_ref[...].astype(jnp.float32)
    for f in range(8):
        rows = mix_ref[pl.ds(f, 256, stride=8), :]
        if f == 0:
            spot = iota((256, 128), 1)
            pieces = jnp.where((spot >= 96) & (spot < 99), rows, 0.0)
            score_ref[0] = jnp.sum(pieces) / valid_ref[0]
        turned = jnp.transpose(rows, (1, 0)).astype(jnp.bfloat16)
        for w in range(3):
            turned_ref[w, 32 * f:32 * f + 32, :] = turned[32 * w:32 * w + 32]
    full, even, odd, _ = picks(codes_ref[0:1, :], codes_ref[1:2, :])
    first = dot(turned_ref[0], full) + dot(turned_ref[2], even)
    second = dot(turned_ref[1], full) + dot(turned_ref[2], odd)
    natural = jnp.concatenate([first, second], axis=1).astype(jnp.bfloat16)
    out_ref[...] = dot(natural, waves_ref[...]).astype(jnp.bfloat16)


def home_call(valid, codes, got, waves):
    vmem = pl.BlockSpec(memory_space=pltpu.VMEM)
    smem = pl.BlockSpec(memory_space=pltpu.SMEM)
    return pl.pallas_call(
        home_kernel,
        out_shape=(
            jax.ShapeDtypeStruct((1,), jnp.float32),
            jax.ShapeDtypeStruct((256, waves.shape[1]), jnp.bfloat16),
        ),
        in_specs=[smem, vmem, vmem, vmem],
        out_specs=(smem, vmem),
        scratch_shapes=[pltpu.VMEM((2048, 128), jnp.float32), pltpu.VMEM((3, 256, 256), jnp.bfloat16)],
        compiler_params=pltpu.CompilerParams(vmem_limit_bytes=20 * 1024 * 1024),
    )(valid, codes, got, waves)


def exchange(rows):
    return lax.all_to_all(rows, both_axes, split_axis=0, concat_axis=0, tiled=True)


def shift_of(order):
    return jnp.where(order >= 368, 0, (368 - order + 15) // 16 * 16)


def ranked(orders):
    rank = jnp.sum((orders[..., None] > orders[..., None, :]).astype(jnp.int32), axis=-1)
    return rank


def exact(equation, left, right):
    return jnp.einsum(equation, left, right, preferred_element_type=jnp.float32).astype(jnp.bfloat16)


def unpacked(grid, legendre, target, owner, cutoff, waves, modes_valid):
    fields, rows = grid.shape[1:3]
    modes, levels = legendre.shape[1:]
    e = lax.axis_index("ens")
    j = lax.axis_index("lat")
    natural = jnp.arange(modes, dtype=jnp.int32)
    place = jnp.arange(256, dtype=jnp.int32)
    full_slots = place // 16 * 24 + place % 16
    half_slots = place // 16 * 24 + 16 + place % 16 // 2
    pick_full = (owner[full_slots][:, None] == natural).astype(jnp.bfloat16)
    pick_half = (owner[half_slots][:, None] == natural).astype(jnp.bfloat16)
    zeros = jnp.zeros_like(pick_full)
    odd = (place % 2 == 1)[:, None]
    pick = jnp.stack([
        jnp.stack([pick_full, zeros], axis=1),
        jnp.stack([zeros, pick_full], axis=1),
        jnp.stack([jnp.where(odd, zeros, pick_half), jnp.where(odd, pick_half, zeros)], axis=1),
    ], axis=1)
    table = waves.reshape(2, modes, -1)
    fourier = exact("cmn,fan->cmfa", table, grid[0])
    fourier = exchange(exact("dwcm,cmfa->dwfa", pick, fourier).reshape(256, 6, 128))
    fourier = fourier.reshape(16, 16, 3, fields, rows)
    bands = lax.dynamic_slice_in_dim(legendre, 2 * e, 2, axis=0)
    pick_orders = jnp.stack([pick_full, pick_half], axis=1)
    weights = exchange(exact("dom,rml->drol", pick_orders, bands).reshape(256, 4, levels))
    weights = weights.reshape(16, rows, 2, levels)
    weights = jnp.stack([weights[:, :, 0], weights[:, :, 0], weights[:, :, 1]], axis=2)
    coeffs = jnp.einsum("jewfa,jawl->ewfl", fourier, weights, preferred_element_type=jnp.float32)

    own = lax.dynamic_slice_in_dim(owner, 24 * j, 24)
    full_rows = lax.dynamic_index_in_dim(target, e, 0, keepdims=False)
    half_rows = lax.dynamic_slice(target, (16 + e // 2, 0, e % 2, 0), (1, fields, 1, levels))[0, :, 0]
    goal = jnp.stack([full_rows[:, 0], full_rows[:, 1], half_rows])
    order = jnp.stack([own[e], own[e], own[16 + e // 2]])[:, None, None]
    level = jnp.arange(levels, dtype=jnp.int32)
    inside = ((level >= order) & (level <= cutoff[None, :, None])).astype(jnp.float32)
    offset = delta_abs * delta_abs
    spread = coeffs[:, None] - coeffs[None]
    height = jnp.sqrt(spread * spread + offset)
    pair_value = jnp.sum(height - delta_abs, axis=1)
    pair_slope = jnp.sum(spread / height, axis=1)
    spread = coeffs - goal
    height = jnp.sqrt(spread * spread + offset)
    score = jnp.sum(inside * ((height - delta_abs) / 16.0 - pair_value / 512.0))
    grad = (inside * (spread / height - pair_slope / 16.0)).astype(jnp.bfloat16)
    score = exchange(jnp.full((256, 1, 128), score, jnp.float32))
    mean_score = (jnp.sum(score[:, 0, 0]) / modes_valid[0]).reshape(1)

    back = exchange(exact("ewfl,jawl->jewfa", grad, weights).reshape(256, 6, 128))
    back = exact("dwcm,dwfa->facm", pick, back.reshape(256, 3, fields, rows))
    return mean_score, exact("facm,cmn->fan", back, table)[None]


def body(grid, legendre, target, owner, cutoff):
    fields, rows, lon_count = grid.shape[1:]
    modes = legendre.shape[1]
    e = lax.axis_index("ens")
    j = lax.axis_index("lat")
    table = wave_table(modes, lon_count).reshape(2 * modes, lon_count)
    waves = jnp.asarray(table)
    turned = jnp.asarray(np.ascontiguousarray(table.T))
    sent, codes = send_call(
        e.reshape(1), owner, grid.reshape(fields * rows, lon_count), turned, legendre
    )
    got = exchange(sent)

    by_lat = owner.reshape(16, 24)
    rank = ranked(by_lat)
    spots = jnp.arange(24, dtype=jnp.int32)
    by_rank = jnp.sum(jnp.where(rank[:, :, None] == spots, by_lat[:, :, None], 0), axis=1)
    long_orders = by_rank[:, 0:16:2]
    short_orders = by_rank[:, 23:15:-1]
    fits = jnp.all(360 + shift_of(short_orders) <= 511 + long_orders)

    own = lax.dynamic_slice_in_dim(owner, 24 * j, 24)
    own_rank = ranked(own)
    is_full = own_rank == e
    is_half = own_rank == 23 - e // 2
    full_order = jnp.sum(jnp.where(is_full, own, 0))
    half_order = jnp.sum(jnp.where(is_half, own, 0))
    shift = shift_of(half_order)
    orders = jnp.stack([full_order, half_order, shift, jnp.max(cutoff)])
    full_slot = jnp.sum(jnp.where(is_full, spots, 0))
    half_slot = jnp.sum(jnp.where(is_half, spots, 0))
    full_rows = lax.dynamic_index_in_dim(target, full_slot, 0, keepdims=False)
    full_rows = jnp.concatenate([full_rows[:, 0], full_rows[:, 1]])
    half_rows = lax.dynamic_slice(target, (half_slot, 0, e % 2, 0), (1, fields, 1, target.shape[3]))
    half_rows = jnp.pad(half_rows[0, :, 0], ((0, 0), (0, 512 - target.shape[3])))
    half_rows = lax.dynamic_slice_in_dim(jnp.concatenate([half_rows, half_rows], axis=1), 512 - shift, 512, axis=1)
    limit = jnp.broadcast_to(cutoff[:, None], (fields, 128))
    cut_level = cutoff.astype(jnp.float32)
    modes_valid = jnp.sum((cut_level + 1.0) * (cut_level + 2.0)).reshape(1)

    flag = fits.astype(jnp.int32)
    got, flag, modes_valid = lax.optimization_barrier((got, flag, modes_valid))
    back = score_call(orders, got, full_rows, half_rows, limit)
    home = exchange(back.reshape(256, 8, 128)).reshape(2048, 128)
    mean_score, grid_grad = home_call(modes_valid, codes, home, waves)
    grid_grad = grid_grad.reshape(1, fields, rows, lon_count)
    _, mean_score, grid_grad = lax.while_loop(
        lambda state: state[0] == 0,
        lambda state: (jnp.int32(1), *unpacked(grid, legendre, target, owner, cutoff, waves, modes_valid)),
        (flag, mean_score, grid_grad),
    )
    return mean_score, grid_grad


def solution(mesh):
    in_specs = (
        P("ens", None, "lat", None),
        P("lat", None, None),
        P("lat", None, None, None),
        P(),
        P(),
    )
    out_specs = (P(), P("ens", None, "lat", None))
    return jax.shard_map(body, mesh=mesh, in_specs=in_specs, out_specs=out_specs, check_vma=False)
```

```python
import math

import jax
import jax.numpy as jnp
import numpy as np
from jax import lax
from jax.experimental import pallas as pl
from jax.experimental.pallas import tpu as pltpu
from jax.sharding import PartitionSpec as P

delta_abs = 0.1
both_axes = ("lat", "ens")


def wave_table(mode_count, lon_count):
    points = np.arange(lon_count, dtype=np.int64)
    modes = np.arange(mode_count, dtype=np.int64)
    phase = modes[:, None] * points[None, :] % lon_count
    angle = phase.astype(np.float32) * np.float32(2.0 * math.pi / lon_count)
    both = np.stack([np.cos(angle), -np.sin(angle)]) / np.float32(math.sqrt(lon_count))
    return both.astype(np.float32).astype(jnp.bfloat16)


def dot(left, right):
    return jnp.dot(left, right, preferred_element_type=jnp.float32)


def flag(condition):
    return jnp.where(condition, 1.0, 0.0).astype(jnp.bfloat16)


def iota(shape, axis):
    return lax.broadcasted_iota(jnp.int32, shape, axis)


def send_kernel(
    place_ref, owner_hbm, grid_hbm, waves_hbm, legendre_hbm, out_ref, codes_ref,
    owner_ref, grid_ref, waves_ref, bands_ref, table_ref, four_ref, mix_ref, sems,
):
    grid_copy = pltpu.make_async_copy(grid_hbm, grid_ref, sems.at[0])
    band_copy = pltpu.make_async_copy(
        legendre_hbm.at[pl.ds(2 * place_ref[0], 2)], bands_ref, sems.at[1]
    )
    wave_copies = [
        pltpu.make_async_copy(
            waves_hbm.at[:, pl.ds(384 * c, 384)], waves_ref.at[:, pl.ds(384 * c, 384)], sems.at[2 + c]
        )
        for c in range(2)
    ]
    owner_copy = pltpu.make_async_copy(owner_hbm, owner_ref, sems.at[4])
    owner_copy.start()
    band_copy.start()
    grid_copy.start()
    for copy in wave_copies:
        copy.start()

    group = flag(iota((16, 384), 1) // 24 == iota((16, 384), 0))
    before = flag(iota((384, 384), 0) < iota((384, 384), 1))
    table_ref[0:384, 384:512] = jnp.zeros((384, 128), jnp.bfloat16)
    codes_ref[2:8, :] = jnp.zeros((6, 384), jnp.float32)
    owner_copy.wait()
    line = jnp.broadcast_to(owner_ref[...].reshape(1, 384).astype(jnp.float32), (128, 384))
    column = jnp.transpose(line, (1, 0))
    lane = iota((384, 128), 1).astype(jnp.float32)
    held = jnp.concatenate([flag(column == lane + 128.0 * t) for t in range(3)], axis=1)
    lat_of = dot(group, held)
    count = dot(lat_of.astype(jnp.bfloat16), before)
    rank = jnp.sum(lat_of * count, axis=0, keepdims=True)
    lat = jnp.sum(lat_of * iota((16, 384), 0).astype(jnp.float32), axis=0, keepdims=True)
    full_code = jnp.where(rank < 16.0, lat * 16.0 + rank, -1.0)
    half_code = jnp.where(rank >= 16.0, lat * 8.0 + (23.0 - rank), -1.0)
    codes_ref[0:1, :] = full_code
    codes_ref[1:2, :] = half_code
    full, even, odd, half = picks(full_code, half_code)

    both = jnp.concatenate([full, half], axis=1)
    band_copy.wait()
    for r in range(2):
        rows = bands_ref[r]
        table_ref[0:384, 0:384] = rows
        wide = jnp.concatenate([rows.astype(jnp.float32), jnp.zeros((384, 128), jnp.float32)], axis=1)
        table_ref[384 + 368:768, :] = wide[368:384].astype(jnp.bfloat16)
        for step in range(1, 24):
            low = 368 - 16 * step
            moved = pltpu.roll(wide[low:low + 16], 16 * step, 1)
            table_ref[384 + low:384 + low + 16, :] = moved.astype(jnp.bfloat16)
        packed = dot(both, table_ref[...])
        for t in range(4):
            mix_ref[3 + t, pl.ds(r, 256, stride=2), :] = packed[:, 128 * t:128 * t + 128]

    for t in range(3, 7):
        out_ref[:, :, 128 * t:128 * t + 128] = mix_ref[t].astype(jnp.bfloat16).reshape(256, 2, 128)

    dims = (((1,), (1,)), ((), ()))
    grid_copy.wait()
    for c in range(2):
        wave_copies[c].wait()
        columns = slice(384 * c, 384 * c + 384)
        four_ref[:, columns] = dot(grid_ref[...], waves_ref[:, columns]).astype(jnp.bfloat16)
        part = lax.dot_general(full, four_ref[:, columns], dims, preferred_element_type=jnp.float32)
        for h in range(2):
            mix_ref[h, pl.ds(c, 256, stride=2), :] = part[:, 128 * h:128 * h + 128]
    part = lax.dot_general(
        jnp.concatenate([even, odd], axis=1), four_ref[...], dims, preferred_element_type=jnp.float32
    )
    for h in range(2):
        mix_ref[2, pl.ds(h, 256, stride=2), :] = part[:, 128 * h:128 * h + 128]
    for t in range(3):
        out_ref[:, :, 128 * t:128 * t + 128] = mix_ref[t].astype(jnp.bfloat16).reshape(256, 2, 128)


def picks(full_code, half_code):
    row = iota((256, 384), 0)
    full = flag(row.astype(jnp.float32) == full_code)
    match = (row // 2).astype(jnp.float32) == half_code
    even = flag(match & (row % 2 == 0))
    odd = flag(match & (row % 2 == 1))
    return full, even, odd, flag(match)


def send_call(place, owner, grid, waves, legendre):
    vmem = pl.BlockSpec(memory_space=pltpu.VMEM)
    anywhere = pl.BlockSpec(memory_space=pltpu.HBM)
    return pl.pallas_call(
        send_kernel,
        out_shape=(
            jax.ShapeDtypeStruct((256, 2, 896), jnp.bfloat16),
            jax.ShapeDtypeStruct((8, 384), jnp.float32),
        ),
        in_specs=[pl.BlockSpec(memory_space=pltpu.SMEM), anywhere, anywhere, anywhere, anywhere],
        out_specs=(vmem, vmem),
        scratch_shapes=[
            pltpu.VMEM((384,), jnp.int32),
            pltpu.VMEM((256, 1440), jnp.bfloat16),
            pltpu.VMEM((1440, 768), jnp.bfloat16),
            pltpu.VMEM((2, 384, 384), jnp.bfloat16),
            pltpu.VMEM((768, 512), jnp.bfloat16),
            pltpu.VMEM((256, 768), jnp.bfloat16),
            pltpu.VMEM((7, 512, 128), jnp.float32),
            pltpu.SemaphoreType.DMA((5,)),
        ],
        compiler_params=pltpu.CompilerParams(vmem_limit_bytes=58 * 1024 * 1024),
    )(place, owner, grid, waves, legendre)


def score_kernel(
    orders_ref, got_ref, full_ref, half_ref, cutoff_ref, back_ref,
    flat_ref, rows_ref, coeffs_ref, grads_ref, total_ref,
):
    flat_ref[...] = got_ref[...].reshape(512, 896)
    lane_group = iota((32, 128), 1) // 32
    for q in range(3):
        for group in range(4):
            blocks = [
                flat_ref[128 * group + 32 * i:128 * group + 32 * i + 32, 128 * q:128 * q + 128].astype(jnp.float32)
                for i in range(4)
            ]
            for k in range(4):
                merged = jnp.zeros((32, 128), jnp.float32)
                for i in range(4):
                    turn = (i - k) % 4
                    block = pltpu.roll(blocks[i], 32 * turn, 1) if turn else blocks[i]
                    merged = jnp.where(lane_group == i, block, merged)
                row = (q * 4 + k) * 32
                rows_ref[row:row + 32, 128 * group:128 * group + 128] = merged.astype(jnp.bfloat16)
    coeffs = dot(rows_ref[...], flat_ref[:, 384:896])
    for t in range(4):
        coeffs_ref[t] = coeffs[:, 128 * t:128 * t + 128]
    offset = delta_abs * delta_abs
    limit = cutoff_ref[...]

    def column(level, order, goal, load, store):
        inside = (level >= order) & (level <= limit)
        member = [load(e) for e in range(16)]
        slope = [jnp.zeros((8, 128), jnp.float32) for _ in range(16)]
        rest = jnp.zeros((8, 128), jnp.float32)
        for i in range(15):
            group = jnp.full((8, 128), (i - 15.0) / delta_abs, jnp.float32)
            for k in range(i + 1, 16):
                spread = member[i] - member[k]
                inverse = lax.rsqrt(spread * spread + offset)
                step_slope = spread * inverse
                slope[i] = slope[i] + step_slope
                slope[k] = slope[k] - step_slope
                group = group + inverse
            rest = rest + group
        pair_value = offset * rest
        for i in range(1, 16):
            pair_value = pair_value + (member[i] - member[0]) * slope[i]
        own_value = jnp.zeros((8, 128), jnp.float32)
        for i in range(16):
            spread = member[i] - goal
            square = spread * spread + offset
            inverse = lax.rsqrt(square)
            own_value = own_value + (square * inverse - delta_abs)
            store(i, jnp.where(inside, spread * inverse - slope[i] / 16.0, 0.0))
        total_ref[...] += jnp.where(inside, own_value / 16.0 - pair_value / 256.0, 0.0)

    total_ref[...] = jnp.zeros((8, 128), jnp.float32)
    full_order, half_order, shift, highest = [orders_ref[i] for i in range(4)]

    def full_step(step):
        part = step // 3
        third = step % 3
        lanes = pl.ds(third * 128, 128)
        first = third * 128
        active = (first + 127 >= full_order) & (first <= highest)

        def load(e):
            return coeffs_ref[third, pl.ds(2 * e + part, 8, stride=32), :]

        def store(e, value):
            grads_ref[pl.ds(part * 128 + 8 * e, 8), lanes] = value

        @pl.when(active)
        def _():
            goal = full_ref[pl.ds(part * 8, 8), lanes]
            column(iota((8, 128), 1) + first, full_order, goal, load, store)

        @pl.when(jnp.logical_not(active))
        def _():
            grads_ref[pl.ds(part * 128, 128), lanes] = jnp.zeros((128, 128), jnp.float32)

    for step in range(6):
        full_step(step)

    @pl.loop(0, 4)
    def _(tile):
        lanes = pl.ds(pl.multiple_of(tile * 128, 128), 128)
        first = tile * 128 - shift
        first = jnp.where(first < 0, first + 512, first)
        active = ((first + 127 >= half_order) & (first <= highest)) | (first - 385 >= half_order)

        def load(e):
            return jnp.concatenate(
                [coeffs_ref[tile, pl.ds(256 + 2 * e + h, 4, stride=32), :] for h in range(2)]
            )

        def store(e, value):
            grads_ref[256 + 8 * e:256 + 8 * e + 8, lanes] = value

        @pl.when(active)
        def _():
            level = iota((8, 128), 1) + first
            level = jnp.where(level >= 512, level - 512, level)
            column(level, half_order, half_ref[:, lanes], load, store)

        @pl.when(jnp.logical_not(active))
        def _():
            grads_ref[256:384, lanes] = jnp.zeros((128, 128), jnp.float32)

    grads_ref[0:256, 384:512] = jnp.zeros((256, 128), jnp.float32)
    total = total_ref[...]
    score = jnp.sum(jnp.sum(total, axis=1, keepdims=True), axis=0, keepdims=True)
    high = score.astype(jnp.bfloat16).astype(jnp.float32)
    middle = (score - high).astype(jnp.bfloat16).astype(jnp.float32)
    low = score - high - middle
    spot = iota((128, 128), 1)
    pieces = jnp.where(spot == 96, high, jnp.where(spot == 97, middle, jnp.where(spot == 98, low, 0.0)))

    waves_grad = lax.dot_general(
        grads_ref[...].astype(jnp.bfloat16), flat_ref[:, 384:896], (((1,), (1,)), ((), ())),
        preferred_element_type=jnp.float32,
    )
    for j in range(16):
        merged = pieces
        for w in range(3):
            block = waves_grad[128 * w:128 * w + 128, 128 * (j // 4):128 * (j // 4) + 128]
            turn = (w - j) % 4
            if turn:
                block = pltpu.roll(block, 32 * turn, 1)
            merged = jnp.where(spot // 32 == w, block, merged)
        back_ref[128 * j:128 * j + 128, :] = merged.astype(jnp.bfloat16)


def score_call(orders, got, full_rows, half_rows, limit):
    vmem = pl.BlockSpec(memory_space=pltpu.VMEM)
    return pl.pallas_call(
        score_kernel,
        out_shape=jax.ShapeDtypeStruct((2048, 128), jnp.bfloat16),
        in_specs=[pl.BlockSpec(memory_space=pltpu.SMEM), vmem, vmem, vmem, vmem],
        out_specs=vmem,
        scratch_shapes=[
            pltpu.VMEM((512, 896), jnp.bfloat16),
            pltpu.VMEM((384, 512), jnp.bfloat16),
            pltpu.VMEM((4, 384, 128), jnp.float32),
            pltpu.VMEM((384, 512), jnp.float32),
            pltpu.VMEM((8, 128), jnp.float32),
        ],
        compiler_params=pltpu.CompilerParams(vmem_limit_bytes=20 * 1024 * 1024),
    )(orders, got, full_rows, half_rows, limit)


def home_kernel(valid_ref, codes_ref, got_ref, waves_ref, score_ref, out_ref, mix_ref, turned_ref):
    mix_ref[...] = got_ref[...].astype(jnp.float32)
    for f in range(8):
        rows = mix_ref[pl.ds(f, 256, stride=8), :]
        if f == 0:
            spot = iota((256, 128), 1)
            pieces = jnp.where((spot >= 96) & (spot < 99), rows, 0.0)
            score_ref[0] = jnp.sum(pieces) / valid_ref[0]
        turned = jnp.transpose(rows, (1, 0)).astype(jnp.bfloat16)
        for w in range(3):
            turned_ref[w, 32 * f:32 * f + 32, :] = turned[32 * w:32 * w + 32]
    full, even, odd, _ = picks(codes_ref[0:1, :], codes_ref[1:2, :])
    first = dot(turned_ref[0], full) + dot(turned_ref[2], even)
    second = dot(turned_ref[1], full) + dot(turned_ref[2], odd)
    natural = jnp.concatenate([first, second], axis=1).astype(jnp.bfloat16)
    out_ref[...] = dot(natural, waves_ref[...]).astype(jnp.bfloat16)


def home_call(valid, codes, got, waves):
    vmem = pl.BlockSpec(memory_space=pltpu.VMEM)
    smem = pl.BlockSpec(memory_space=pltpu.SMEM)
    return pl.pallas_call(
        home_kernel,
        out_shape=(
            jax.ShapeDtypeStruct((1,), jnp.float32),
            jax.ShapeDtypeStruct((256, waves.shape[1]), jnp.bfloat16),
        ),
        in_specs=[smem, vmem, vmem, vmem],
        out_specs=(smem, vmem),
        scratch_shapes=[pltpu.VMEM((2048, 128), jnp.float32), pltpu.VMEM((3, 256, 256), jnp.bfloat16)],
        compiler_params=pltpu.CompilerParams(vmem_limit_bytes=20 * 1024 * 1024),
    )(valid, codes, got, waves)


def exchange(rows):
    return lax.all_to_all(rows, both_axes, split_axis=0, concat_axis=0, tiled=True)


def shift_of(order):
    return jnp.where(order >= 368, 0, (368 - order + 15) // 16 * 16)


def ranked(orders):
    rank = jnp.sum((orders[..., None] > orders[..., None, :]).astype(jnp.int32), axis=-1)
    return rank


def exact(equation, left, right):
    return jnp.einsum(equation, left, right, preferred_element_type=jnp.float32).astype(jnp.bfloat16)


def unpacked(grid, legendre, target, owner, cutoff, waves, modes_valid):
    fields, rows = grid.shape[1:3]
    modes, levels = legendre.shape[1:]
    e = lax.axis_index("ens")
    j = lax.axis_index("lat")
    natural = jnp.arange(modes, dtype=jnp.int32)
    place = jnp.arange(256, dtype=jnp.int32)
    full_slots = place // 16 * 24 + place % 16
    half_slots = place // 16 * 24 + 16 + place % 16 // 2
    pick_full = (owner[full_slots][:, None] == natural).astype(jnp.bfloat16)
    pick_half = (owner[half_slots][:, None] == natural).astype(jnp.bfloat16)
    zeros = jnp.zeros_like(pick_full)
    odd = (place % 2 == 1)[:, None]
    pick = jnp.stack([
        jnp.stack([pick_full, zeros], axis=1),
        jnp.stack([zeros, pick_full], axis=1),
        jnp.stack([jnp.where(odd, zeros, pick_half), jnp.where(odd, pick_half, zeros)], axis=1),
    ], axis=1)
    table = waves.reshape(2, modes, -1)
    fourier = exact("cmn,fan->cmfa", table, grid[0])
    fourier = exchange(exact("dwcm,cmfa->dwfa", pick, fourier).reshape(256, 6, 128))
    fourier = fourier.reshape(16, 16, 3, fields, rows)
    bands = lax.dynamic_slice_in_dim(legendre, 2 * e, 2, axis=0)
    pick_orders = jnp.stack([pick_full, pick_half], axis=1)
    weights = exchange(exact("dom,rml->drol", pick_orders, bands).reshape(256, 4, levels))
    weights = weights.reshape(16, rows, 2, levels)
    weights = jnp.stack([weights[:, :, 0], weights[:, :, 0], weights[:, :, 1]], axis=2)
    coeffs = jnp.einsum("jewfa,jawl->ewfl", fourier, weights, preferred_element_type=jnp.float32)

    own = lax.dynamic_slice_in_dim(owner, 24 * j, 24)
    full_rows = lax.dynamic_index_in_dim(target, e, 0, keepdims=False)
    half_rows = lax.dynamic_slice(target, (16 + e // 2, 0, e % 2, 0), (1, fields, 1, levels))[0, :, 0]
    goal = jnp.stack([full_rows[:, 0], full_rows[:, 1], half_rows])
    order = jnp.stack([own[e], own[e], own[16 + e // 2]])[:, None, None]
    level = jnp.arange(levels, dtype=jnp.int32)
    inside = ((level >= order) & (level <= cutoff[None, :, None])).astype(jnp.float32)
    offset = delta_abs * delta_abs
    spread = coeffs[:, None] - coeffs[None]
    height = jnp.sqrt(spread * spread + offset)
    pair_value = jnp.sum(height - delta_abs, axis=1)
    pair_slope = jnp.sum(spread / height, axis=1)
    spread = coeffs - goal
    height = jnp.sqrt(spread * spread + offset)
    score = jnp.sum(inside * ((height - delta_abs) / 16.0 - pair_value / 512.0))
    grad = (inside * (spread / height - pair_slope / 16.0)).astype(jnp.bfloat16)
    score = exchange(jnp.full((256, 1, 128), score, jnp.float32))
    mean_score = (jnp.sum(score[:, 0, 0]) / modes_valid[0]).reshape(1)

    back = exchange(exact("ewfl,jawl->jewfa", grad, weights).reshape(256, 6, 128))
    back = exact("dwcm,dwfa->facm", pick, back.reshape(256, 3, fields, rows))
    return mean_score, exact("facm,cmn->fan", back, table)[None]


def body(grid, legendre, target, owner, cutoff):
    fields, rows, lon_count = grid.shape[1:]
    modes = legendre.shape[1]
    e = lax.axis_index("ens")
    j = lax.axis_index("lat")
    table = wave_table(modes, lon_count).reshape(2 * modes, lon_count)
    waves = jnp.asarray(table)
    turned = jnp.asarray(np.ascontiguousarray(table.T))
    sent, codes = send_call(
        e.reshape(1), owner, grid.reshape(fields * rows, lon_count), turned, legendre
    )
    got = exchange(sent)

    by_lat = owner.reshape(16, 24)
    rank = ranked(by_lat)
    spots = jnp.arange(24, dtype=jnp.int32)
    by_rank = jnp.sum(jnp.where(rank[:, :, None] == spots, by_lat[:, :, None], 0), axis=1)
    long_orders = by_rank[:, 0:16:2]
    short_orders = by_rank[:, 23:15:-1]
    fits = jnp.all(360 + shift_of(short_orders) <= 511 + long_orders)

    own = lax.dynamic_slice_in_dim(owner, 24 * j, 24)
    own_rank = ranked(own)
    is_full = own_rank == e
    is_half = own_rank == 23 - e // 2
    full_order = jnp.sum(jnp.where(is_full, own, 0))
    half_order = jnp.sum(jnp.where(is_half, own, 0))
    shift = shift_of(half_order)
    orders = jnp.stack([full_order, half_order, shift, jnp.max(cutoff)])
    full_slot = jnp.sum(jnp.where(is_full, spots, 0))
    half_slot = jnp.sum(jnp.where(is_half, spots, 0))
    full_rows = lax.dynamic_index_in_dim(target, full_slot, 0, keepdims=False)
    full_rows = jnp.concatenate([full_rows[:, 0], full_rows[:, 1]])
    half_rows = lax.dynamic_slice(target, (half_slot, 0, e % 2, 0), (1, fields, 1, target.shape[3]))
    half_rows = jnp.pad(half_rows[0, :, 0], ((0, 0), (0, 512 - target.shape[3])))
    half_rows = lax.dynamic_slice_in_dim(jnp.concatenate([half_rows, half_rows], axis=1), 512 - shift, 512, axis=1)
    limit = jnp.broadcast_to(cutoff[:, None], (fields, 128))
    cut_level = cutoff.astype(jnp.float32)
    modes_valid = jnp.sum((cut_level + 1.0) * (cut_level + 2.0)).reshape(1)

    flag = fits.astype(jnp.int32)
    got, flag, modes_valid = lax.optimization_barrier((got, flag, modes_valid))
    back = score_call(orders, got, full_rows, half_rows, limit)
    home = exchange(back.reshape(256, 8, 128)).reshape(2048, 128)
    mean_score, grid_grad = home_call(modes_valid, codes, home, waves)
    grid_grad = grid_grad.reshape(1, fields, rows, lon_count)
    _, mean_score, grid_grad = lax.while_loop(
        lambda state: state[0] == 0,
        lambda state: (jnp.int32(1), *unpacked(grid, legendre, target, owner, cutoff, waves, modes_valid)),
        (flag, mean_score, grid_grad),
    )
    return mean_score, grid_grad


def solution(mesh):
    in_specs = (
        P("ens", None, "lat", None),
        P("lat", None, None),
        P("lat", None, None, None),
        P(),
        P(),
    )
    out_specs = (P(), P("ens", None, "lat", None))
    return jax.shard_map(body, mesh=mesh, in_specs=in_specs, out_specs=out_specs, check_vma=False)
```
